256 devices in a mesh: gx: 32 (over x, z_hi, y), gy: 8 (over z_lo, core).
Axes of the slice: x: 4, y: 4, z: 8 (z_hi: 2, z_lo: 4; z = z_hi * 4 + z_lo), core: 2. Of those that a mesh axis runs over, the one named last changes fastest.
Arguments:
- moisture_ratio: float32 [1024, 512, 128], P('gx', 'gy'), may hold values from 9 to 12
- kelvin_warmth: float32 [1024, 512, 128], P('gx', 'gy'), may hold values from 284 to 292
- wind_ratio_east: float32 [1024, 512, 128], P('gx', 'gy'), may hold values from 0.05 to 0.35
- wind_ratio_north: float32 [1024, 512, 128], P('gx', 'gy'), may hold values from 0.05 to 0.35
- parcel_particles: float32 [524288, 3, 128], P(('gx', 'gy')), as said below
- parcel_home_region: int32 [524288], P(('gx', 'gy')), may hold values from 0 to 4095
- leaving_parcel_places: int32 [32, 8, 8, 64], P('gx', 'gy'), may hold values from 0 to 2047, as said below
- sending_tallies: int32 [32, 8, 8], P('gx', 'gy'), may hold values from 0 to 64, as said below
Outputs:
- moisture_ratio_later: float32 [1024, 512, 128], P('gx', 'gy')
- kelvin_warmth_later: float32 [1024, 512, 128], P('gx', 'gy')
- droplets_out: float32 [524288, 3, 128], P(('gx', 'gy'))
- incoming_parcels: float32 [32, 8, 8, 64, 3, 128], P('gx', 'gy')
The draws below stay inside these ranges and needn't reach their ends.
Inputs may be any that keep to these rules, and one draw needn't show every extreme that they name: `leaving_parcel_places`: on each device the 512 entries are distinct local droplet-block indices. `sending_tallies`: each device has one direction with exactly 64 live slots. `parcel_particles`: radius 1 to 15, multiplicity 1 to 10, solute 0.1 to 1.
All inputs are finite; a program needn't handle non-finite values.
Results may differ from the reference program's by a relative error of at most 0.0003.
Values sent between devices are 32-bit elements; how exact they have to be, the bound alone decides.
No kernel may reach another device: no remote copies, remote signals or barrier semaphores. Data moves between devices by JAX's collectives and lax.ppermute only.
A program may use at most 128 MiB of HBM per device.

```python
import math
import jax
import jax.numpy as jnp
import numpy as np
from jax import lax

CX = 32
CY = 64
HEIGHT_LAYERS = 128
NB = 2048
SLOTS = 64
WIDTH_EAST_WEST = 1024
WIDTH_NORTH_SOUTH = 512
CELL_BLOCKS = 4096
BLOCKS_ALL = 524288
N_GX = 32
N_GY = 8


def draw_parcel_particles(key, part):
    keys = jax.random.split(jax.random.fold_in(key, 11), 3)
    bounds = [(1.0, 15.0), (1.0, 10.0), (0.1, 1.0)]
    parts_list = []
    for index in range(3):
        low, high = bounds[index]
        values = jnp.exp(jax.random.uniform(keys[index], (BLOCKS_ALL, 128), jnp.float32, jnp.log(low), jnp.log(high)))
        parts_list.append(values)
    return jnp.stack(parts_list, axis=1).astype(jnp.float32)


def draw_leaving_parcel_places(key, part):
    keys = jax.random.split(jax.random.fold_in(key, 23), N_GX * N_GY)
    picks = jax.vmap(lambda single: jax.random.permutation(single, NB)[:8 * SLOTS])(keys)
    return picks.reshape(N_GX, N_GY, 8, SLOTS).astype(jnp.int32)


def draw_sending_tallies(key, part):
    first = jax.random.fold_in(key, 31)
    second = jax.random.fold_in(key, 37)
    base = jax.random.randint(first, (N_GX, N_GY, 8), 0, SLOTS + 1)
    full_dir = jax.random.randint(second, (N_GX, N_GY), 0, 8)
    return jnp.where(jnp.arange(8)[None, None, :] == full_dir[..., None], SLOTS, base).astype(jnp.int32)


def set_ends(array, rng, low, largest):
    shape = array.shape
    place = [jax.random.randint(jax.random.fold_in(rng, axis), (), 0, shape[axis]) for axis in range(len(shape))]
    array = array.at[tuple(place)].set(low)
    longest = shape.index(max(shape))
    place[longest] = (place[longest] + 1) % shape[longest]
    return array.at[tuple(place)].set(largest)


def shard_levels(rng, extent, cuts, low, high):
    gain = 1.0
    for dim, blocks in cuts:
        steps = jax.random.uniform(jax.random.fold_in(jax.random.fold_in(rng, 6), dim), (blocks,), jnp.float32, low / len(cuts), high / len(cuts))
        gain = gain * jnp.repeat(jnp.exp(steps), extent[dim] // blocks).reshape((-1,) + (1,) * (len(extent) - 1 - dim))
    return gain


def cumulative_ranks(count, lean):
    loads = [(1 << 20) // math.isqrt(grade ** lean) + 1 for grade in range(1, count + 1)]
    deviation = 1 + sum(loads) // (1 << 30)
    return np.cumsum(np.array([max(1, weight // deviation) for weight in loads]))


def skewed_ids(key, shape, number_of, slope):
    grid = cumulative_ranks(number_of, slope)
    ticket = jax.random.randint(jax.random.fold_in(key, 1), shape, 0, int(grid[number_of - 1]))
    standing = jnp.searchsorted(jnp.asarray(grid, jnp.int32), ticket, side="right")
    return jax.random.permutation(jax.random.fold_in(key, 2), number_of)[standing].astype(jnp.int32)


def setup_inputs(seed: int = 0) -> dict:
    splits = jax.random.split(jax.random.key(seed), 9)
    return {
        "moisture_ratio": jnp.clip(9.0 + 3.0 * jax.random.uniform(splits[0], (WIDTH_EAST_WEST, WIDTH_NORTH_SOUTH, HEIGHT_LAYERS), jnp.float32) ** shard_levels(splits[0], (WIDTH_EAST_WEST, WIDTH_NORTH_SOUTH, HEIGHT_LAYERS), ((0, 32), (1, 8)), -0.2, 0.2), 9.0, 12.0),
        "kelvin_warmth": jnp.clip(284.0 + 8.0 * jax.random.uniform(splits[1], (WIDTH_EAST_WEST, WIDTH_NORTH_SOUTH, HEIGHT_LAYERS), jnp.float32) ** shard_levels(splits[1], (WIDTH_EAST_WEST, WIDTH_NORTH_SOUTH, HEIGHT_LAYERS), ((0, 32), (1, 8)), -0.2, 0.2), 284.0, 292.0),
        "wind_ratio_east": jnp.clip(0.05 + 0.29999999 * jax.random.uniform(splits[2], (WIDTH_EAST_WEST, WIDTH_NORTH_SOUTH, HEIGHT_LAYERS), jnp.float32) ** shard_levels(splits[2], (WIDTH_EAST_WEST, WIDTH_NORTH_SOUTH, HEIGHT_LAYERS), ((0, 32), (1, 8)), -0.2, 0.2), 0.05, 0.35),
        "wind_ratio_north": jnp.clip(0.05 + 0.29999999 * jax.random.uniform(splits[3], (WIDTH_EAST_WEST, WIDTH_NORTH_SOUTH, HEIGHT_LAYERS), jnp.float32) ** shard_levels(splits[3], (WIDTH_EAST_WEST, WIDTH_NORTH_SOUTH, HEIGHT_LAYERS), ((0, 32), (1, 8)), -0.2, 0.2), 0.05, 0.35),
        "parcel_particles": draw_parcel_particles(jax.random.fold_in(splits[8], 71), 0),
        "parcel_home_region": set_ends(skewed_ids(splits[5], (BLOCKS_ALL,), CELL_BLOCKS, 2), jax.random.fold_in(splits[5], 3), 0, CELL_BLOCKS - 1).astype(jnp.int32),
        "leaving_parcel_places": draw_leaving_parcel_places(jax.random.fold_in(splits[8], 71), 0),
        "sending_tallies": draw_sending_tallies(jax.random.fold_in(splits[8], 71), 0),
    }


diffusion = 0.1
growth = 20.0
curvature = 0.01
floor_sq = 0.25
mass_unit = 0.0003
release_warmth = 2.5

def saturation(temp):
    return 3.8 * jnp.exp(17.27 * (temp - 273.15) / (temp - 35.86))

def transport(field, from_west, from_east, from_south, from_north, wind_ratio_east, wind_ratio_north):
    return field - wind_ratio_east * (field - from_west) - wind_ratio_north * (field - from_south) + diffusion * (from_west + from_east + from_south + from_north - 4.0 * field)

def grow(fetched, parcel_particles):
    vap_cells = jnp.concatenate([fetched[:, :64], fetched[:, :64]], axis=1)
    temp_cells = jnp.concatenate([fetched[:, 64:], fetched[:, 64:]], axis=1)
    supersat = vap_cells / saturation(temp_cells) - 1.0
    radius = parcel_particles[:, 0]
    multiple = parcel_particles[:, 1]
    solute = parcel_particles[:, 2]
    cubed = radius * radius * radius
    square = jnp.maximum(radius * radius + growth * (supersat - curvature / radius + solute / cubed), floor_sq)
    new_radius = jnp.sqrt(square)
    condensed = multiple * (new_radius * new_radius * new_radius - cubed) * mass_unit
    return (jnp.stack([new_radius, multiple, solute], axis=1), condensed)

def grow_by_uptake(moisture_regions, warmth_regions, parcel_particles, parcel_home_region):
    parcel_region_table = jnp.concatenate([moisture_regions, warmth_regions], axis=1)
    onehot = (parcel_home_region[:, None] == jnp.arange(moisture_regions.shape[0], dtype=jnp.int32)[None, :]).astype(jnp.float32)
    fetched = jnp.dot(onehot, parcel_region_table, precision=lax.Precision.HIGHEST)
    revised_particles, condensed = grow(fetched, parcel_particles)
    place_parcels_home = lax.dot_general(onehot, condensed, (((0,), (0,)), ((), ())), precision=lax.Precision.HIGHEST)
    place_parcels_home = place_parcels_home[:, :64] + place_parcels_home[:, 64:]
    return (moisture_regions - place_parcels_home, warmth_regions + release_warmth * place_parcels_home, revised_particles)

def reference(moisture_ratio, kelvin_warmth, wind_ratio_east, wind_ratio_north, parcel_particles, parcel_home_region, leaving_parcel_places, sending_tallies):

    def carry_tracers_by_wind(field):
        return transport(field, jnp.roll(field, 1, 0), jnp.roll(field, -1, 0), jnp.roll(field, 1, 1), jnp.roll(field, -1, 1), wind_ratio_east, wind_ratio_north)

    def split_to_regions(field):
        return field.reshape(N_GX, CX, N_GY, CY, HEIGHT_LAYERS).transpose(0, 2, 1, 3, 4).reshape(N_GX * N_GY, CELL_BLOCKS, 64)

    def from_blocks(blocks):
        return blocks.reshape(N_GX, N_GY, CX, CY, HEIGHT_LAYERS).transpose(0, 2, 1, 3, 4).reshape(WIDTH_EAST_WEST, WIDTH_NORTH_SOUTH, HEIGHT_LAYERS)
    moisture_regions = split_to_regions(carry_tracers_by_wind(moisture_ratio))
    warmth_regions = split_to_regions(carry_tracers_by_wind(kelvin_warmth))
    particles_on_unit = parcel_particles.reshape(N_GX * N_GY, NB, 3, 128)
    labels_on_unit = parcel_home_region.reshape(N_GX * N_GY, NB)

    def solitary_unit(items):
        return grow_by_uptake(items[0], items[1], items[2], items[3])
    fresh_moisture, fresh_warmth, revised_particles = lax.map(solitary_unit, (moisture_regions, warmth_regions, particles_on_unit, labels_on_unit))
    lists = leaving_parcel_places.reshape(N_GX * N_GY, 8 * SLOTS).astype(jnp.int32)
    payload = jax.vmap(lambda block, picks: block[picks])(revised_particles, lists)
    payload = payload.reshape(N_GX, N_GY, 8, SLOTS, 3, 128)
    live = (jnp.arange(SLOTS, dtype=jnp.int32)[None, None, None, :] < sending_tallies[..., None]).astype(jnp.float32)
    payload = payload * live[..., None, None]
    moves = [(1, 0), (-1, 0), (0, 1), (0, -1), (1, 1), (1, -1), (-1, 1), (-1, -1)]
    arrived = [jnp.roll(jnp.roll(payload[:, :, d], moves[d][0], 0), moves[d][1], 1) for d in range(8)]
    incoming_parcels = jnp.stack(arrived, axis=2)
    return (from_blocks(fresh_moisture), from_blocks(fresh_warmth), revised_particles.reshape(BLOCKS_ALL, 3, 128), incoming_parcels)
```

```python
import jax
import jax.numpy as jnp
from jax import lax
from jax.experimental import pallas as pl
from jax.experimental.pallas import tpu as pltpu
from jax.sharding import PartitionSpec as P

CX, CY, LEV = 32, 64, 128
ROWS = CX * CY
NB = 2048
SLOTS = 64
CHUNKS = 8
CROWS = ROWS // CHUNKS
LANES_ACC = 4
F32 = jnp.float32
ANY = pl.BlockSpec(memory_space=pltpu.HBM)
VM = pl.BlockSpec(memory_space=pltpu.VMEM)
SM = pl.BlockSpec(memory_space=pltpu.SMEM)


EAST, WEST, NORTH, SOUTH = (0, 4, 5), (1, 6, 7), (2, 4, 6), (3, 5, 7)


def supersat(q, t):
    return q * jnp.exp(-17.27 * (t - 273.15) / (t - 35.86)) * (1.0 / 3.8) - 1.0


def both_halves(s):
    low = lax.broadcasted_iota(jnp.int32, s.shape, 1) < 64
    turned = pltpu.roll(s, 64, 1)
    return jnp.where(low, s, turned), jnp.where(low, turned, s)


def growth_base(r, sol):
    inv = 1.0 / r
    return r * r + 20.0 * (sol * (inv * inv * inv) - 0.01 * inv)


def fetch_rows(count, place, pairs, step=8):
    def group(g, _):
        slots = [g * step + u for u in range(step)]
        rows = [place(s) for s in slots]
        values = [[src[pl.ds(row, 1)] for row in rows] for src, _ in pairs]
        for (_, dst), column in zip(pairs, values):
            for s, value in zip(slots, column):
                dst[pl.ds(s, 1)] = value
        return 0

    lax.fori_loop(0, count // step, group, 0)


def odd_x():
    return lax.rem(lax.axis_index("gx"), 2) == 1


def odd_y():
    return lax.rem(lax.axis_index("gy"), 2) == 1


def kernel_edges(q_h, t_h, xa, xb, ya, yb, slabs, tiles, xsem, ysem):
    copies = []
    for f, src in enumerate((q_h, t_h)):
        for side in range(2):
            copies.append(pltpu.make_async_copy(
                src.at[:, pl.ds((CY - 8) * side, 8)], tiles.at[f, side], ysem.at[f, side]))
            copies.append(pltpu.make_async_copy(
                src.at[(CX - 1) * side], slabs.at[f, side], xsem.at[f, side]))
    for c in copies:
        c.start()
    for c in copies:
        c.wait()
    ox, oy = odd_x(), odd_y()
    for f in range(2):
        low, high = slabs[f, 0], slabs[f, 1]
        xa[f] = jnp.where(ox, low, high)
        xb[f] = jnp.where(ox, high, low)
        low, high = tiles[f, 0, :, 0, :], tiles[f, 1, :, 7, :]
        ya[f] = jnp.where(oy, low, high)
        yb[f] = jnp.where(oy, high, low)


def kernel_advect(
    places, q_h, t_h, we_h, wn_h, parts_h,
    aq, at, table, pv, cw, cs, leave,
    qv, tv, wev, wnv, sems, psem,
):
    fields = ((q_h, qv), (t_h, tv), (we_h, wev), (wn_h, wnv))
    copies = [
        [
            pltpu.make_async_copy(
                src.at[pl.ds(k * CROWS, CROWS)], dst.at[pl.ds(k * CROWS, CROWS)], sems.at[f, k]
            )
            for f, (src, dst) in enumerate(fields)
        ]
        for k in range(CHUNKS)
    ]
    for row in copies:
        for c in row:
            c.start()
    pcopies = [pltpu.make_async_copy(parts_h.at[p], pv.at[p], psem.at[p]) for p in range(3)]
    for c in pcopies:
        c.start()
    yi = lax.broadcasted_iota(jnp.int32, (CY, LEV), 0)
    first, last = yi == 0, yi == CY - 1
    kn = jnp.where(last, 0.0, 0.1).astype(F32)

    def slab(x, _):
        r0 = pl.multiple_of(x * CY, CY)
        rw = pl.multiple_of(jnp.maximum(x - 1, 0) * CY, CY)
        re = pl.multiple_of(jnp.minimum(x + 1, CX - 1) * CY, CY)
        here = pl.ds(r0, CY)
        we, wn = wev[here], wnv[here]
        mid = 0.6 - we - wn
        kw = (we + 0.1) * jnp.where(x > 0, 1.0, 0.0)
        ks = jnp.where(first, 0.0, wn + 0.1)
        ke = jnp.where(x < CX - 1, 0.1, 0.0)

        def carried(v):
            f = v[here]
            return (
                mid * f
                + kw * v[pl.ds(rw, CY)]
                + ks * pltpu.roll(f, 1, 0)
                + ke * v[pl.ds(re, CY)]
                + kn * pltpu.roll(f, CY - 1, 0)
            )

        q, t = carried(qv), carried(tv)
        aq[here] = q
        at[here] = t
        even, odd = both_halves(supersat(q, t))
        table[pl.ds(2 * r0, CY, stride=2)] = even
        table[pl.ds(2 * r0 + 1, CY, stride=2)] = odd
        return 0

    per = CX // CHUNKS
    for k in range(CHUNKS):
        if k == 0:
            copies[0][0].wait()
            copies[0][1].wait()
        copies[k][2].wait()
        copies[k][3].wait()
        if k + 1 < CHUNKS:
            copies[k + 1][0].wait()
            copies[k + 1][1].wait()
        lax.fori_loop(k * per, (k + 1) * per, slab, 0)
    cw[...] = wev[0:CY] + 0.1
    cs[...] = wnv[pl.ds(0, CX, stride=CY)] + 0.1
    for c in pcopies:
        c.wait()
    for d in (0, 4, 5, 1, 6, 7):
        fetch_rows(
            SLOTS, lambda s, d=d: places[0, 0, d, s], [(pv.at[p], leave.at[d, p]) for p in range(3)]
        )


def kernel_fix(
    places, tallies, home, hxa, hxb, hya, hyb, cw, cs, leave, aq_in, at_in, table_in,
    aq, at, table, send_a, send_b, got,
):
    ox, oy = odd_x(), odd_y()
    for f, a in ((0, aq), (1, at)):
        a[0:CY] += cw[...] * jnp.where(ox, hxa[f], hxb[f])
        a[ROWS - CY : ROWS] += 0.1 * jnp.where(ox, hxb[f], hxa[f])
        a[pl.ds(0, CX, stride=CY)] += cs[...] * jnp.where(oy, hya[f], hyb[f])
        a[pl.ds(CY - 1, CX, stride=CY)] += 0.1 * jnp.where(oy, hyb[f], hya[f])

    def refresh(rows, start, count, stride):
        even, odd = both_halves(supersat(aq[rows], at[rows]))
        table[pl.ds(2 * start, count, stride=2 * stride)] = even
        table[pl.ds(2 * start + 1, count, stride=2 * stride)] = odd

    refresh(pl.ds(0, CY), 0, CY, 1)
    refresh(pl.ds(ROWS - CY, CY), ROWS - CY, CY, 1)
    refresh(pl.ds(0, CX, stride=CY), 0, CX, CY)
    refresh(pl.ds(CY - 1, CX, stride=CY), CY - 1, CX, CY)
    slot = lax.broadcasted_iota(jnp.int32, (SLOTS, LEV), 0)
    for send, odd in ((send_a, ox), (send_b, jnp.logical_not(ox))):
        for n in range(3):
            d = jnp.where(odd, WEST[n], EAST[n])
            fetch_rows(SLOTS, lambda s, d=d: home[places[0, 0, d, s]], [(table, got)])
            live = slot < tallies[0, 0, d]
            square = growth_base(leave[d, 0], leave[d, 2]) + 20.0 * got[...]
            send[n, 0] = jnp.where(live, jnp.sqrt(jnp.maximum(square, 0.25)), 0.0)
            send[n, 1] = jnp.where(live, leave[d, 1], 0.0)
            send[n, 2] = jnp.where(live, leave[d, 2], 0.0)


def kernel_grow(places, tallies, home, table, pv, parts_out, cond, ahead, got, new_r, sems, psem):
    copies = [pltpu.make_async_copy(pv.at[p], parts_out.at[p], psem.at[p]) for p in (1, 2)]
    for c in copies:
        c.start()
    outs = []
    per = NB // CHUNKS
    for k in range(CHUNKS):
        fetch_rows(per, lambda s, k=k: home[k * per + s], [(table, got.at[k % 2])], 16)

        def grow(g, _, k=k):
            here = pl.ds(pl.multiple_of(g * 64, 64), 64)
            rows = pl.ds(pl.multiple_of(k * per + g * 64, 64), 64)
            r, m = pv[0, rows], pv[1, rows]
            square = growth_base(r, pv[2, rows]) + 20.0 * got[k % 2, here]
            square = jnp.maximum(square, 0.25)
            new = jnp.sqrt(square)
            new_r[rows] = new
            cond[rows] = (0.0003 * m) * (square * new - r * r * r)
            return 0

        lax.fori_loop(0, per // 64, grow, 0)
        c = pltpu.make_async_copy(
            new_r.at[pl.ds(k * per, per)], parts_out.at[0, pl.ds(k * per, per)], sems.at[k]
        )
        c.start()
        outs.append(c)
    slot = lax.broadcasted_iota(jnp.int32, (SLOTS, LEV), 0)
    for n, d in enumerate((2, 3)):
        fetch_rows(
            SLOTS,
            lambda s, d=d: places[0, 0, d, s],
            [(new_r, ahead.at[n, 0]), (pv.at[1], ahead.at[n, 1]), (pv.at[2], ahead.at[n, 2])],
        )
        live = slot < tallies[0, 0, d]
        for p in range(3):
            ahead[n, p] = jnp.where(live, ahead[n, p], 0.0)
    for c in outs + copies:
        c.wait()


def kernel_forward(ahead, xa, xb, ya, yb):
    ox, oy = odd_x(), odd_y()
    for n in range(3):
        for p in range(3):
            if n == 0:
                up, down = ahead[0, p], ahead[1, p]
            else:
                one, two = (xa, xb) if n == 1 else (xb, xa)
                up = jnp.where(ox, one[1, p], two[1, p])
                down = jnp.where(ox, one[2, p], two[2, p])
            ya[n, p] = jnp.where(oy, down, up)
            yb[n, p] = jnp.where(oy, up, down)


def kernel_deposit(home, cond, aq, at, q_out, t_out, acc, qo, to, sems):
    def clear(g, _):
        for k in range(LANES_ACC):
            acc[k, pl.ds(pl.multiple_of(g * 128, 128), 128)] = jnp.zeros((128, LEV), F32)
        return 0

    lax.fori_loop(0, 2 * ROWS // 128, clear, 0)

    def scatter(g, _):
        b0 = g * LANES_ACC
        at_rows = [home[b0 + k] for k in range(LANES_ACC)]
        sums = [acc[k, pl.ds(at_rows[k], 1)] + cond[pl.ds(b0 + k, 1)] for k in range(LANES_ACC)]
        for k in range(LANES_ACC):
            acc[k, pl.ds(at_rows[k], 1)] = sums[k]
        return 0

    lax.fori_loop(0, NB // LANES_ACC, scatter, 0, unroll=4)
    low = lax.broadcasted_iota(jnp.int32, (64, LEV), 1) < 64
    outs = []
    for j in range(CHUNKS):

        def gather(g, _, j=j):
            r0 = pl.multiple_of(j * CROWS + g * 64, 64)
            rows = pl.ds(r0, 64)
            even, odd = pl.ds(2 * r0, 64, stride=2), pl.ds(2 * r0 + 1, 64, stride=2)
            x0, x1 = acc[0, even], acc[0, odd]
            for k in range(1, LANES_ACC):
                x0, x1 = x0 + acc[k, even], x1 + acc[k, odd]
            dep = jnp.where(low, x0, x1) + pltpu.roll(jnp.where(low, x1, x0), 64, 1)
            qo[rows] = aq[rows] - dep
            to[rows] = at[rows] + 2.5 * dep
            return 0

        lax.fori_loop(0, CROWS // 64, gather, 0)
        for n, (src, dst) in enumerate(((qo, q_out), (to, t_out))):
            rows = pl.ds(j * CROWS, CROWS)
            c = pltpu.make_async_copy(src.at[rows], dst.at[rows], sems.at[n, j])
            c.start()
            outs.append(c)
    for c in outs:
        c.wait()


def kernel_arrive(xa, xb, ya, yb, out, buf, sems):
    ox, oy = odd_x(), odd_y()
    sources = {0: (xa, xb, 0, ox), 1: (xb, xa, 0, ox)}
    for n in range(3):
        sources[NORTH[n]] = (ya, yb, n, oy)
        sources[SOUTH[n]] = (yb, ya, n, oy)
    copies = []
    for d, (one, two, n, odd) in sources.items():
        buf[d] = jnp.where(odd, one[n], two[n])
        copies.append(pltpu.make_async_copy(buf.at[d], out.at[d], sems.at[d]))
        copies[-1].start()
    for c in copies:
        c.wait()


def vmem(*shape):
    return pltpu.VMEM(shape, F32)


def hbm(*shape):
    return pltpu.HBM(shape, F32)


def in_hbm(x):
    return pltpu.with_memory_space_constraint(x, pltpu.HBM)


def dma(*shape):
    return pltpu.SemaphoreType.DMA(shape)


def call(kernel, name, us, ins, outs, shapes, scratch, aliases=None, mib=24):
    return pl.pallas_call(
        kernel,
        in_specs=ins,
        out_specs=outs,
        out_shape=shapes,
        scratch_shapes=scratch,
        input_output_aliases=aliases or {},
        compiler_params=pltpu.CompilerParams(vmem_limit_bytes=mib << 20),
        cost_estimate=pl.CostEstimate(flops=0, bytes_accessed=int(us * 3.0e6), transcendentals=0),
        name=name,
    )


def swapped(value, axis, phase):
    count = lax.axis_size(axis)
    step = [1 if (i + phase) % 2 == 0 else -1 for i in range(count)]
    return lax.ppermute(value, axis, [(i, (i + step[i]) % count) for i in range(count)])


def body(q, t, we, wn, parts, home, places, tallies):
    parts = in_hbm(parts.transpose(1, 0, 2))
    pay = vmem(3, 3, SLOTS, LEV)
    xa, xb, ya, yb = call(
        kernel_edges, "edge_columns", 1, [ANY] * 2, [VM] * 4,
        [vmem(2, CY, LEV)] * 2 + [vmem(2, CX, LEV)] * 2,
        [vmem(2, 2, CY, LEV), vmem(2, 2, CX, 8, LEV), dma(2, 2), dma(2, 2)],
    )(in_hbm(q), in_hbm(t))
    hxb = swapped(xb, "gx", 1)
    hxa = swapped(xa, "gx", 0)
    hyb = swapped(yb, "gy", 1)
    hya = swapped(ya, "gy", 0)
    flat = [in_hbm(x.reshape(ROWS, LEV)) for x in (q, t, we, wn)]
    cells, table_of = vmem(ROWS, LEV), vmem(2 * ROWS, LEV)
    aq, at, table, pv, cw, cs, leave = call(
        kernel_advect, "advect", 5, [SM] + [ANY] * 5, [VM] * 7,
        [cells, cells, table_of, vmem(3, NB, LEV), vmem(CY, LEV), vmem(CX, LEV), vmem(8, 3, SLOTS, LEV)],
        [cells] * 4 + [dma(4, CHUNKS), dma(3)],
    )(places, *flat, parts)
    aq, at, table, sa, sb = call(
        kernel_fix, "fix_edges", 1, [SM] * 3 + [VM] * 10, [VM] * 5,
        [cells, cells, table_of, pay, pay], [vmem(SLOTS, LEV)], {10: 0, 11: 1, 12: 2},
    )(places, tallies, home, hxa, hxb, hya, hyb, cw, cs, leave, aq, at, table)
    gxb = swapped(sb, "gx", 1)
    gxa = swapped(sa, "gx", 0)
    parts_out, cond, ahead = call(
        kernel_grow, "grow", 6, [SM] * 3 + [VM] * 2, [ANY, VM, VM],
        [hbm(3, NB, LEV), vmem(NB, LEV), vmem(2, 3, SLOTS, LEV)],
        [vmem(2, NB // CHUNKS, LEV), vmem(NB, LEV), dma(CHUNKS), dma(2 + 1)],
    )(places, tallies, home, table, pv)
    ya, yb = call(kernel_forward, "forward", 1, [VM] * 3, [VM] * 2, [pay, pay], [])(ahead, gxa, gxb)
    gyb = swapped(yb, "gy", 1)
    gya = swapped(ya, "gy", 0)
    q_out, t_out = call(
        kernel_deposit, "deposit", 6, [SM] + [VM] * 3, [ANY, ANY],
        [hbm(ROWS, LEV), hbm(ROWS, LEV)],
        [vmem(LANES_ACC, 2 * ROWS, LEV), cells, cells, dma(2, CHUNKS)],
    )(home, cond, aq, at)
    arrived = call(
        kernel_arrive, "arrive", 1, [VM] * 4, ANY, hbm(8, 3, SLOTS, LEV),
        [vmem(8, 3, SLOTS, LEV), dma(8)],
    )(gxa, gxb, gya, gyb)
    incoming = arrived.transpose(0, 2, 1, 3)[None, None]
    shape = (CX, CY, LEV)
    return q_out.reshape(shape), t_out.reshape(shape), parts_out.transpose(1, 0, 2), incoming


def solution(mesh):
    cells = P("gx", "gy", None)
    blocks = P(("gx", "gy"), None, None)
    return jax.shard_map(
        body,
        mesh=mesh,
        in_specs=(cells, cells, cells, cells, blocks, P(("gx", "gy")),
                  P("gx", "gy", None, None), P("gx", "gy", None)),
        out_specs=(cells, cells, blocks, P("gx", "gy", None, None, None, None)),
        check_vma=False,
    )
```

```python
import math

import jax
import jax.numpy as jnp
from jax import lax
from jax.experimental import pallas as pl
from jax.experimental.pallas import tpu as pltpu
from jax.sharding import PartitionSpec as P

CX, CY, LEV = 32, 64, 128
ROWS = CX * CY
NB = 2048
SLOTS = 64
CHUNKS = 8
CROWS = ROWS // CHUNKS
LANES_ACC = 4
UNROLL = 8
POWER = 17.27 * (273.15 - 35.86) * math.log2(math.e)
SHIFT = 17.27 * math.log2(math.e) + math.log2(3.8)
F32 = jnp.float32
ANY = pl.BlockSpec(memory_space=pltpu.HBM)
VM = pl.BlockSpec(memory_space=pltpu.VMEM)
SM = pl.BlockSpec(memory_space=pltpu.SMEM)


EAST, WEST, NORTH, SOUTH = (0, 4, 5), (1, 6, 7), (2, 4, 6), (3, 5, 7)


def supersat(q, t):
    return q * jnp.exp2(POWER / (t - 35.86) - SHIFT) - 1.0


def both_halves(s):
    low = lax.broadcasted_iota(jnp.int32, s.shape, 1) < 64
    turned = pltpu.roll(s, 64, 1)
    return jnp.where(low, s, turned), jnp.where(low, turned, s)


def root(x):
    return x * lax.rsqrt(x)


def growth_base(r, sol):
    inv = 1.0 / r
    return r * r + 20.0 * (sol * (inv * inv * inv) - 0.01 * inv)


def fetch_rows(count, place, pairs, step=64):
    def group(g, _):
        slots = [g * step + u for u in range(step)]
        rows = [place(s) for s in slots]
        values = [[src[pl.ds(row, 1)] for row in rows] for src, _ in pairs]
        for (_, dst), column in zip(pairs, values):
            for s, value in zip(slots, column):
                dst[pl.ds(s, 1)] = value
        return 0

    lax.fori_loop(0, count // step, group, 0)


def odd_x():
    return lax.rem(lax.axis_index("gx"), 2) == 1


def odd_y():
    return lax.rem(lax.axis_index("gy"), 2) == 1


def gx_sends(sends):
    ox = odd_x()
    for send, odd in zip(sends, (jnp.logical_not(ox), ox)):
        for n in range(3):
            yield send, n, jnp.where(odd, WEST[n], EAST[n])


def kernel_send(
    q_h, t_h, places_h, tallies_h, parts_h, xb, xa, yb, ya, rest,
    slabs, tiles, places, tallies, xsem, ysem, sems,
):
    copies = []
    for f, src in enumerate((q_h, t_h)):
        for side in range(2):
            copies.append(pltpu.make_async_copy(
                src.at[:, pl.ds((CY - 8) * side, 8)], tiles.at[f, side], ysem.at[f, side]))
            copies.append(pltpu.make_async_copy(
                src.at[(CX - 1) * side], slabs.at[f, side], xsem.at[f, side]))
    copies.append(pltpu.make_async_copy(places_h, places, sems.at[0]))
    copies.append(pltpu.make_async_copy(tallies_h, tallies, sems.at[1]))
    planes = [pltpu.make_async_copy(parts_h.at[1 + p], rest.at[p], sems.at[2 + p]) for p in range(2)]
    for c in copies + planes:
        c.start()
    for c in copies:
        c.wait()
    ox, oy = odd_x(), odd_y()
    for f in range(2):
        low, high = slabs[f, 0], slabs[f, 1]
        xa[f] = jnp.where(ox, low, high)
        xb[f] = jnp.where(ox, high, low)
        low, high = tiles[f, 0, :, 0, :], tiles[f, 1, :, 7, :]
        ya[f] = jnp.where(oy, low, high)
        yb[f] = jnp.where(oy, high, low)
    slot = lax.broadcasted_iota(jnp.int32, (SLOTS, LEV), 0)
    for p in range(2):
        planes[p].wait()
        for send, n, d in gx_sends((xb, xa)):
            dst = send.at[2 + 2 * n + p]
            fetch_rows(SLOTS, lambda s, d=d: places[0, 0, d, s], [(rest.at[p], dst)])
            dst[...] = jnp.where(slot < tallies[0, 0, d], dst[...], 0.0)


def stencil(fields, sems, outs):
    aq, at, table = outs
    per = CX // CHUNKS
    copies = {
        (f, k): pltpu.make_async_copy(
            src.at[pl.ds(k * CROWS, CROWS)], dst.at[pl.ds(k * CROWS, CROWS)], sems.at[f, k]
        )
        for k in range(CHUNKS)
        for f, (src, dst) in enumerate(fields)
    }
    for c in copies.values():
        c.start()
    (_, qv), (_, tv), (_, wev), (_, wnv) = fields
    yi = lax.broadcasted_iota(jnp.int32, (CY, LEV), 0)
    first, last = yi == 0, yi == CY - 1
    kn = jnp.where(last, 0.0, 0.1).astype(F32)

    def slab(x, _):
        r0 = pl.multiple_of(x * CY, CY)
        rw = pl.multiple_of(jnp.maximum(x - 1, 0) * CY, CY)
        re = pl.multiple_of(jnp.minimum(x + 1, CX - 1) * CY, CY)
        here = pl.ds(r0, CY)
        we, wn = wev[here], wnv[here]
        mid = 0.6 - we - wn
        kw = (we + 0.1) * jnp.where(x > 0, 1.0, 0.0)
        ks = jnp.where(first, 0.0, wn + 0.1)
        ke = jnp.where(x < CX - 1, 0.1, 0.0)

        def carried(v):
            f = v[here]
            return (
                mid * f
                + kw * v[pl.ds(rw, CY)]
                + ks * pltpu.roll(f, 1, 0)
                + ke * v[pl.ds(re, CY)]
                + kn * pltpu.roll(f, CY - 1, 0)
            )

        q, t = carried(qv), carried(tv)
        aq[here] = q
        at[here] = t
        even, odd = both_halves(supersat(q, t))
        table[pl.ds(2 * r0, CY, stride=2)] = even
        table[pl.ds(2 * r0 + 1, CY, stride=2)] = odd
        return 0

    waited = set()

    def wait(*keys):
        for key in keys:
            if key in copies and key not in waited:
                copies[key].wait()
                waited.add(key)

    for k in range(CHUNKS):
        wait(*[(f, j) for j in (k - 1, k, k + 1) for f in range(2)], (2, k), (3, k))
        lax.fori_loop(k * per, (k + 1) * per, slab, 0, unroll=4)


def kernel_advect(
    places_h, q_h, t_h, we_h, wn_h, parts_h,
    aq, at, table, cw, cs, radius, leave_b, leave_a,
    qv, tv, wev, wnv, places, sems, psem,
):
    copies = [
        pltpu.make_async_copy(places_h, places, psem.at[0]),
        pltpu.make_async_copy(parts_h.at[0], radius, psem.at[1]),
    ]
    for c in copies:
        c.start()
    stencil(((q_h, qv), (t_h, tv), (we_h, wev), (wn_h, wnv)), sems, (aq, at, table))
    cw[...] = wev[0:CY] + 0.1
    cs[...] = wnv[pl.ds(0, CX, stride=CY)] + 0.1
    for c in copies:
        c.wait()
    for leave, n, d in gx_sends((leave_b, leave_a)):
        fetch_rows(SLOTS, lambda s, d=d: places[0, 0, d, s], [(radius, leave.at[n])])


def kernel_fix(
    places_h, tallies_h, home_h, hxb, hxa, hyb, hya, cw, cs, leave_b, leave_a, xb, xa, aq_in, at_in, table_in,
    aq, at, table, send_b, send_a, got, places, tallies, home, sems,
):
    lists = ((places_h, places), (tallies_h, tallies), (home_h, home))
    copies = [pltpu.make_async_copy(a, b, sems.at[k]) for k, (a, b) in enumerate(lists)]
    for c in copies:
        c.start()
    ox, oy = odd_x(), odd_y()
    for f, a in ((0, aq), (1, at)):
        a[0:CY] += cw[...] * jnp.where(ox, hxa[f], hxb[f])
        a[ROWS - CY : ROWS] += 0.1 * jnp.where(ox, hxb[f], hxa[f])
        a[pl.ds(0, CX, stride=CY)] += cs[...] * jnp.where(oy, hya[f], hyb[f])
        a[pl.ds(CY - 1, CX, stride=CY)] += 0.1 * jnp.where(oy, hyb[f], hya[f])

    def refresh(rows, start, count, stride):
        even, odd = both_halves(supersat(aq[rows], at[rows]))
        table[pl.ds(2 * start, count, stride=2 * stride)] = even
        table[pl.ds(2 * start + 1, count, stride=2 * stride)] = odd

    refresh(pl.ds(0, CY), 0, CY, 1)
    refresh(pl.ds(ROWS - CY, CY), ROWS - CY, CY, 1)
    refresh(pl.ds(0, CX, stride=CY), 0, CX, CY)
    refresh(pl.ds(CY - 1, CX, stride=CY), CY - 1, CX, CY)
    for c in copies:
        c.wait()
    slot = lax.broadcasted_iota(jnp.int32, (SLOTS, LEV), 0)
    radii, rests = (leave_b, leave_a), (xb, xa)
    for k, (send, n, d) in enumerate(gx_sends((send_b, send_a))):
        fetch_rows(SLOTS, lambda s, d=d: home[places[0, 0, d, s]], [(table, got)])
        square = growth_base(radii[k // 3][n], rests[k // 3][3 + 2 * n]) + 20.0 * got[...]
        send[n] = jnp.where(slot < tallies[0, 0, d], root(jnp.maximum(square, 0.25)), 0.0)


def kernel_grow(places, tallies, home, table, radius, rest, parts_out, cond, ahead, got, new_r, sems, psem):
    copies = [pltpu.make_async_copy(rest.at[p], parts_out.at[1 + p], psem.at[p]) for p in range(2)]
    for c in copies:
        c.start()
    outs = []
    per = NB // CHUNKS
    for k in range(CHUNKS):
        fetch_rows(per, lambda s, k=k: home[k * per + s], [(table, got.at[k % 2])])

        def grow(g, _, k=k):
            here = pl.ds(pl.multiple_of(g * 64, 64), 64)
            rows = pl.ds(pl.multiple_of(k * per + g * 64, 64), 64)
            r, m = radius[rows], rest[0, rows]
            square = growth_base(r, rest[1, rows]) + 20.0 * got[k % 2, here]
            square = jnp.maximum(square, 0.25)
            new = root(square)
            new_r[rows] = new
            taken = (0.0003 * m) * (square * new - r * r * r)
            cond[rows] = taken + pltpu.roll(taken, 64, 1)
            return 0

        lax.fori_loop(0, per // 64, grow, 0, unroll=4)
        c = pltpu.make_async_copy(
            new_r.at[pl.ds(k * per, per)], parts_out.at[0, pl.ds(k * per, per)], sems.at[k]
        )
        c.start()
        outs.append(c)
    slot = lax.broadcasted_iota(jnp.int32, (SLOTS, LEV), 0)
    for n, d in enumerate((2, 3)):
        fetch_rows(
            SLOTS,
            lambda s, d=d: places[0, 0, d, s],
            [(new_r, ahead.at[n, 0]), (rest.at[0], ahead.at[n, 1]), (rest.at[1], ahead.at[n, 2])],
        )
        live = slot < tallies[0, 0, d]
        for p in range(3):
            ahead[n, p] = jnp.where(live, ahead[n, p], 0.0)
    for c in outs + copies:
        c.wait()


def piece(radius, rest, n, p):
    return radius[n] if p == 0 else rest[1 + 2 * n + p]


def kernel_forward(ahead, ra, rb, ma, mb, ya, yb):
    ox, oy = odd_x(), odd_y()
    a, b = (ra, ma), (rb, mb)
    for n in range(3):
        for p in range(3):
            if n == 0:
                up, down = ahead[0, p], ahead[1, p]
            else:
                one, two = (a, b) if n == 1 else (b, a)
                up = jnp.where(ox, piece(*one, 1, p), piece(*two, 1, p))
                down = jnp.where(ox, piece(*one, 2, p), piece(*two, 2, p))
            ya[n, p] = jnp.where(oy, down, up)
            yb[n, p] = jnp.where(oy, up, down)


def kernel_deposit(home, cond, aq, at, q_out, t_out, acc, qo, to, sems):
    def clear(g, _):
        for k in range(LANES_ACC):
            acc[k, pl.ds(pl.multiple_of(g * 128, 128), 128)] = jnp.zeros((128, LEV), F32)
        return 0

    lax.fori_loop(0, ROWS // 128, clear, 0)
    half = lax.broadcasted_iota(jnp.int32, (1, LEV), 1) // 64

    def scatter(g, _):
        b0 = g * LANES_ACC
        where = [home[b0 + k] for k in range(LANES_ACC)]
        rows = [pl.ds(c >> 1, 1) for c in where]
        sums = [
            acc[k, rows[k]] + jnp.where(half == (where[k] & 1), cond[pl.ds(b0 + k, 1)], 0.0)
            for k in range(LANES_ACC)
        ]
        for k in range(LANES_ACC):
            acc[k, rows[k]] = sums[k]
        return 0

    lax.fori_loop(0, NB // LANES_ACC, scatter, 0, unroll=UNROLL)
    outs = []
    for j in range(CHUNKS):

        def gather(g, _, j=j):
            rows = pl.ds(pl.multiple_of(j * CROWS + g * 64, 64), 64)
            dep = acc[0, rows]
            for k in range(1, LANES_ACC):
                dep = dep + acc[k, rows]
            qo[rows] = aq[rows] - dep
            to[rows] = at[rows] + 2.5 * dep
            return 0

        lax.fori_loop(0, CROWS // 64, gather, 0)
        for n, (src, dst) in enumerate(((qo, q_out), (to, t_out))):
            rows = pl.ds(j * CROWS, CROWS)
            c = pltpu.make_async_copy(src.at[rows], dst.at[rows], sems.at[n, j])
            c.start()
            outs.append(c)
    for c in outs:
        c.wait()


def kernel_arrive(ra, rb, ma, mb, ya, yb, out, buf, sems):
    ox, oy = odd_x(), odd_y()
    copies = []

    def ship(d):
        copies.append(pltpu.make_async_copy(buf.at[d], out.at[d], sems.at[d]))
        copies[-1].start()

    for d, one, two in ((0, (ra, ma), (rb, mb)), (1, (rb, mb), (ra, ma))):
        for p in range(3):
            buf[d, p] = jnp.where(ox, piece(*one, 0, p), piece(*two, 0, p))
        ship(d)
    for n in range(3):
        for d, one, two in ((NORTH[n], ya, yb), (SOUTH[n], yb, ya)):
            buf[d] = jnp.where(oy, one[n], two[n])
            ship(d)
    for c in copies:
        c.wait()


def vmem(*shape):
    return pltpu.VMEM(shape, F32)


def hbm(*shape):
    return pltpu.HBM(shape, F32)


def in_hbm(x):
    return pltpu.with_memory_space_constraint(x, pltpu.HBM)


def dma(*shape):
    return pltpu.SemaphoreType.DMA(shape)


def call(kernel, name, us, ins, outs, shapes, scratch, aliases=None, mib=24):
    return pl.pallas_call(
        kernel,
        in_specs=ins,
        out_specs=outs,
        out_shape=shapes,
        scratch_shapes=scratch,
        input_output_aliases=aliases or {},
        compiler_params=pltpu.CompilerParams(vmem_limit_bytes=mib << 20),
        cost_estimate=pl.CostEstimate(flops=0, bytes_accessed=int(us * 3.0e6), transcendentals=0),
        name=name,
    )


def swapped(value, axis, phase):
    count = lax.axis_size(axis)
    step = [1 if (i + phase) % 2 == 0 else -1 for i in range(count)]
    return lax.ppermute(value, axis, [(i, (i + step[i]) % count) for i in range(count)])


def body(q, t, we, wn, parts, home, places, tallies):
    parts = in_hbm(parts.transpose(1, 0, 2))
    q_h, t_h = in_hbm(q), in_hbm(t)
    flat = [in_hbm(x.reshape(ROWS, LEV)) for x in (q, t, we, wn)]
    places_h, tallies_h, home_h = in_hbm(places), in_hbm(tallies), in_hbm(home)
    places_s, tallies_s = pltpu.SMEM((1, 1, 8, SLOTS), jnp.int32), pltpu.SMEM((1, 1, 8), jnp.int32)
    cells, table_of, blocks = vmem(ROWS, LEV), vmem(2 * ROWS, LEV), vmem(NB, LEV)
    pay, radii = vmem(3, 3, SLOTS, LEV), vmem(3, SLOTS, LEV)
    xb, xa, yb, ya, rest = call(
        kernel_send, "send_edges", 1, [ANY] * 5, [VM] * 5,
        [vmem(8, CY, LEV)] * 2 + [vmem(2, CX, LEV)] * 2 + [vmem(2, NB, LEV)],
        [vmem(2, 2, CY, LEV), vmem(2, 2, CX, 8, LEV), places_s, tallies_s, dma(2, 2), dma(2, 2), dma(4)],
    )(q_h, t_h, places_h, tallies_h, parts)
    hxb = swapped(xb, "gx", 1)
    hxa = swapped(xa, "gx", 0)
    hyb = swapped(yb, "gy", 1)
    hya = swapped(ya, "gy", 0)
    aq, at, table, cw, cs, radius, leave_b, leave_a = call(
        kernel_advect, "advect", 6, [ANY] * 6, [VM] * 8,
        [cells, cells, table_of, vmem(CY, LEV), vmem(CX, LEV), blocks, radii, radii],
        [cells] * 4 + [places_s, dma(4, CHUNKS), dma(2)],
    )(places_h, *flat, parts)
    aq, at, table, rb, ra = call(
        kernel_fix, "fix_edges", 1, [ANY] * 3 + [VM] * 13, [VM] * 5,
        [cells, cells, table_of, radii, radii],
        [vmem(SLOTS, LEV), places_s, tallies_s, pltpu.SMEM((NB,), jnp.int32), dma(3)],
        {13: 0, 14: 1, 15: 2},
    )(places_h, tallies_h, home_h, hxb, hxa, hyb, hya, cw, cs, leave_b, leave_a, xb, xa, aq, at, table)
    rb = swapped(rb, "gx", 1)
    ra = swapped(ra, "gx", 0)
    parts_out, cond, ahead = call(
        kernel_grow, "grow", 6, [SM] * 3 + [VM] * 3, [ANY, VM, VM],
        [hbm(3, NB, LEV), blocks, vmem(2, 3, SLOTS, LEV)],
        [vmem(2, NB // CHUNKS, LEV), blocks, dma(CHUNKS), dma(2)],
    )(places, tallies, home, table, radius, rest)
    ya, yb = call(kernel_forward, "forward", 1, [VM] * 5, [VM] * 2, [pay, pay], [])(ahead, ra, rb, hxa, hxb)
    gyb = swapped(yb, "gy", 1)
    gya = swapped(ya, "gy", 0)
    q_out, t_out = call(
        kernel_deposit, "deposit", 6, [SM] + [VM] * 3, [ANY, ANY],
        [hbm(ROWS, LEV), hbm(ROWS, LEV)],
        [vmem(LANES_ACC, ROWS, LEV), cells, cells, dma(2, CHUNKS)],
    )(home, cond, aq, at)
    arrived = call(
        kernel_arrive, "arrive", 1, [VM] * 6, ANY, hbm(8, 3, SLOTS, LEV),
        [vmem(8, 3, SLOTS, LEV), dma(8)],
    )(ra, rb, hxa, hxb, gya, gyb)
    incoming = arrived.transpose(0, 2, 1, 3)[None, None]
    shape = (CX, CY, LEV)
    return q_out.reshape(shape), t_out.reshape(shape), parts_out.transpose(1, 0, 2), incoming


def solution(mesh):
    cells = P("gx", "gy", None)
    blocks = P(("gx", "gy"), None, None)
    return jax.shard_map(
        body,
        mesh=mesh,
        in_specs=(cells, cells, cells, cells, blocks, P(("gx", "gy")),
                  P("gx", "gy", None, None), P("gx", "gy", None)),
        out_specs=(cells, cells, blocks, P("gx", "gy", None, None, None, None)),
        check_vma=False,
    )
```

```python
import math

import jax
import jax.numpy as jnp
from jax import lax
from jax.experimental import pallas as pl
from jax.experimental.pallas import tpu as pltpu
from jax.sharding import PartitionSpec as P

CX, CY, LEV = 32, 64, 128
ROWS = CX * CY
NB = 2048
SLOTS = 64
CHUNKS = 8
CROWS = ROWS // CHUNKS
LANES_ACC = 4
UNROLL = 8
FIRST = 1024
POWER = 17.27 * (273.15 - 35.86) * math.log2(math.e)
SHIFT = 17.27 * math.log2(math.e) + math.log2(3.8)
F32 = jnp.float32
ANY = pl.BlockSpec(memory_space=pltpu.HBM)
VM = pl.BlockSpec(memory_space=pltpu.VMEM)
SM = pl.BlockSpec(memory_space=pltpu.SMEM)


EAST, WEST, NORTH, SOUTH = (0, 4, 5), (1, 6, 7), (2, 4, 6), (3, 5, 7)


def supersat(q, t):
    return q * jnp.exp2(POWER / (t - 35.86) - SHIFT) - 1.0


def both_halves(s):
    low = lax.broadcasted_iota(jnp.int32, s.shape, 1) < 64
    turned = pltpu.roll(s, 64, 1)
    return jnp.where(low, s, turned), jnp.where(low, turned, s)


def root(x):
    return x * lax.rsqrt(x)


def growth_base(r, sol):
    inv = 1.0 / r
    return r * r + 20.0 * (sol * (inv * inv * inv) - 0.01 * inv)


def fetch_rows(count, place, pairs, step=64):
    def group(g, _):
        slots = [g * step + u for u in range(step)]
        rows = [place(s) for s in slots]
        values = [[src[pl.ds(row, 1)] for row in rows] for src, _ in pairs]
        for (_, dst), column in zip(pairs, values):
            for s, value in zip(slots, column):
                dst[pl.ds(s, 1)] = value
        return 0

    lax.fori_loop(0, count // step, group, 0)


def odd_x():
    return lax.rem(lax.axis_index("gx"), 2) == 1


def odd_y():
    return lax.rem(lax.axis_index("gy"), 2) == 1


def gx_sends(sends):
    ox = odd_x()
    for send, odd in zip(sends, (jnp.logical_not(ox), ox)):
        for n in range(3):
            yield send, n, jnp.where(odd, WEST[n], EAST[n])


def kernel_send(
    q_h, t_h, places_h, tallies_h, parts_h, xb, xa, yb, ya, rest,
    slabs, tiles, places, tallies, xsem, ysem, sems,
):
    copies = []
    for f, src in enumerate((q_h, t_h)):
        for side in range(2):
            copies.append(pltpu.make_async_copy(
                src.at[:, pl.ds((CY - 8) * side, 8)], tiles.at[f, side], ysem.at[f, side]))
            copies.append(pltpu.make_async_copy(
                src.at[(CX - 1) * side], slabs.at[f, side], xsem.at[f, side]))
    copies.append(pltpu.make_async_copy(places_h, places, sems.at[0]))
    copies.append(pltpu.make_async_copy(tallies_h, tallies, sems.at[1]))
    planes = [pltpu.make_async_copy(parts_h.at[1 + p], rest.at[p], sems.at[2 + p]) for p in range(2)]
    for c in copies + planes:
        c.start()
    for c in copies:
        c.wait()
    ox, oy = odd_x(), odd_y()
    for f in range(2):
        low, high = slabs[f, 0], slabs[f, 1]
        xa[f] = jnp.where(ox, low, high)
        xb[f] = jnp.where(ox, high, low)
        low, high = tiles[f, 0, :, 0, :], tiles[f, 1, :, 7, :]
        ya[f] = jnp.where(oy, low, high)
        yb[f] = jnp.where(oy, high, low)
    slot = lax.broadcasted_iota(jnp.int32, (SLOTS, LEV), 0)
    for p in range(2):
        planes[p].wait()
        for send, n, d in gx_sends((xb, xa)):
            dst = send.at[2 + 2 * n + p]
            fetch_rows(SLOTS, lambda s, d=d: places[0, 0, d, s], [(rest.at[p], dst)])
            dst[...] = jnp.where(slot < tallies[0, 0, d], dst[...], 0.0)


def stencil(fields, sems, outs):
    aq, at, table = outs
    per = CX // CHUNKS
    copies = {
        (f, k): pltpu.make_async_copy(
            src.at[pl.ds(k * CROWS, CROWS)], dst.at[pl.ds(k * CROWS, CROWS)], sems.at[f, k]
        )
        for k in range(CHUNKS)
        for f, (src, dst) in enumerate(fields)
    }
    for c in copies.values():
        c.start()
    (_, qv), (_, tv), (_, wev), (_, wnv) = fields
    yi = lax.broadcasted_iota(jnp.int32, (CY, LEV), 0)
    first, last = yi == 0, yi == CY - 1
    kn = jnp.where(last, 0.0, 0.1).astype(F32)

    def slab(x, _):
        r0 = pl.multiple_of(x * CY, CY)
        rw = pl.multiple_of(jnp.maximum(x - 1, 0) * CY, CY)
        re = pl.multiple_of(jnp.minimum(x + 1, CX - 1) * CY, CY)
        here = pl.ds(r0, CY)
        we, wn = wev[here], wnv[here]
        mid = 0.6 - we - wn
        kw = (we + 0.1) * jnp.where(x > 0, 1.0, 0.0)
        ks = jnp.where(first, 0.0, wn + 0.1)
        ke = jnp.where(x < CX - 1, 0.1, 0.0)

        def carried(v):
            f = v[here]
            return (
                mid * f
                + kw * v[pl.ds(rw, CY)]
                + ks * pltpu.roll(f, 1, 0)
                + ke * v[pl.ds(re, CY)]
                + kn * pltpu.roll(f, CY - 1, 0)
            )

        q, t = carried(qv), carried(tv)
        aq[here] = q
        at[here] = t
        even, odd = both_halves(supersat(q, t))
        table[pl.ds(2 * r0, CY, stride=2)] = even
        table[pl.ds(2 * r0 + 1, CY, stride=2)] = odd
        return 0

    waited = set()

    def wait(*keys):
        for key in keys:
            if key in copies and key not in waited:
                copies[key].wait()
                waited.add(key)

    for k in range(CHUNKS):
        wait(*[(f, j) for j in (k - 1, k, k + 1) for f in range(2)], (2, k), (3, k))
        lax.fori_loop(k * per, (k + 1) * per, slab, 0, unroll=4)


def kernel_advect(
    places_h, tallies_h, rest, q_h, t_h, we_h, wn_h, parts_h,
    aq, at, table, cw, cs, radius, leave_b, leave_a, along_y,
    qv, tv, wev, wnv, places, tallies, sems, psem,
):
    copies = [
        pltpu.make_async_copy(places_h, places, psem.at[0]),
        pltpu.make_async_copy(tallies_h, tallies, psem.at[2]),
        pltpu.make_async_copy(parts_h.at[0], radius, psem.at[1]),
    ]
    for c in copies:
        c.start()
    stencil(((q_h, qv), (t_h, tv), (we_h, wev), (wn_h, wnv)), sems, (aq, at, table))
    cw[...] = wev[0:CY] + 0.1
    cs[...] = wnv[pl.ds(0, CX, stride=CY)] + 0.1
    for c in copies:
        c.wait()
    for leave, n, d in gx_sends((leave_b, leave_a)):
        fetch_rows(SLOTS, lambda s, d=d: places[0, 0, d, s], [(radius, leave.at[n])])
    slot = lax.broadcasted_iota(jnp.int32, (SLOTS, LEV), 0)
    for n, d in enumerate((2, 3)):
        for p in range(2):
            dst = along_y.at[n, p]
            fetch_rows(SLOTS, lambda s, d=d: places[0, 0, d, s], [(rest.at[p], dst)])
            dst[...] = jnp.where(slot < tallies[0, 0, d], dst[...], 0.0)


def steer(sends, place, north, south, of_b, of_a):
    ox, oy = odd_x(), odd_y()
    for n in range(3):
        if n == 0:
            up, down = north, south
        else:
            one, two = (of_a, of_b) if n == 1 else (of_b, of_a)
            up = jnp.where(ox, one(1), two(1))
            down = jnp.where(ox, one(2), two(2))
        sends[0][place(n)] = jnp.where(oy, up, down)
        sends[1][place(n)] = jnp.where(oy, down, up)


def scatter_rows(home, cond, acc, start, stop):
    half = lax.broadcasted_iota(jnp.int32, (1, LEV), 1) // 64

    def scatter(g, _):
        b0 = g * LANES_ACC
        where = [home[b0 + k] for k in range(LANES_ACC)]
        rows = [pl.ds(c >> 1, 1) for c in where]
        sums = [
            acc[k, rows[k]] + jnp.where(half == (where[k] & 1), cond[pl.ds(b0 + k, 1)], 0.0)
            for k in range(LANES_ACC)
        ]
        for k in range(LANES_ACC):
            acc[k, rows[k]] = sums[k]
        return 0

    lax.fori_loop(start // LANES_ACC, stop // LANES_ACC, scatter, 0, unroll=UNROLL)


def kernel_fix(
    places_h, tallies_h, home_h, hxb, hxa, hyb, hya, cw, cs, leave_b, leave_a, xb, xa, along_y, aq_in, at_in, table_in,
    aq, at, table, send_b, send_a, rest_b, rest_a, got, places, tallies, home, sems,
):
    lists = ((places_h, places), (tallies_h, tallies), (home_h, home))
    copies = [pltpu.make_async_copy(a, b, sems.at[k]) for k, (a, b) in enumerate(lists)]
    for c in copies:
        c.start()
    ox, oy = odd_x(), odd_y()
    for f, a in ((0, aq), (1, at)):
        a[0:CY] += cw[...] * jnp.where(ox, hxa[f], hxb[f])
        a[ROWS - CY : ROWS] += 0.1 * jnp.where(ox, hxb[f], hxa[f])
        a[pl.ds(0, CX, stride=CY)] += cs[...] * jnp.where(oy, hya[f], hyb[f])
        a[pl.ds(CY - 1, CX, stride=CY)] += 0.1 * jnp.where(oy, hyb[f], hya[f])

    def refresh(rows, start, count, stride):
        even, odd = both_halves(supersat(aq[rows], at[rows]))
        table[pl.ds(2 * start, count, stride=2 * stride)] = even
        table[pl.ds(2 * start + 1, count, stride=2 * stride)] = odd

    refresh(pl.ds(0, CY), 0, CY, 1)
    refresh(pl.ds(ROWS - CY, CY), ROWS - CY, CY, 1)
    refresh(pl.ds(0, CX, stride=CY), 0, CX, CY)
    refresh(pl.ds(CY - 1, CX, stride=CY), CY - 1, CX, CY)
    for c in copies:
        c.wait()
    slot = lax.broadcasted_iota(jnp.int32, (SLOTS, LEV), 0)
    radii, rests = (leave_b, leave_a), (xb, xa)
    for k, (send, n, d) in enumerate(gx_sends((send_b, send_a))):
        fetch_rows(SLOTS, lambda s, d=d: home[places[0, 0, d, s]], [(table, got)])
        square = growth_base(radii[k // 3][n], rests[k // 3][3 + 2 * n]) + 20.0 * got[...]
        send[n] = jnp.where(slot < tallies[0, 0, d], root(jnp.maximum(square, 0.25)), 0.0)
    for p in range(2):
        steer(
            (rest_b, rest_a), lambda n, p=p: 2 * n + p, along_y[0, p], along_y[1, p],
            lambda n, p=p: hxb[2 + 2 * n + p], lambda n, p=p: hxa[2 + 2 * n + p],
        )


def kernel_grow(places, tallies, home, table, radius, rest, parts_out, cond, ahead, acc, got, new_r, sems, psem):
    copies = [pltpu.make_async_copy(rest.at[p], parts_out.at[1 + p], psem.at[p]) for p in range(2)]
    for c in copies:
        c.start()
    outs = []
    per = NB // CHUNKS
    for k in range(CHUNKS):
        fetch_rows(per, lambda s, k=k: home[k * per + s], [(table, got.at[k % 2])])

        def grow(g, _, k=k):
            here = pl.ds(pl.multiple_of(g * 64, 64), 64)
            rows = pl.ds(pl.multiple_of(k * per + g * 64, 64), 64)
            r, m = radius[rows], rest[0, rows]
            square = growth_base(r, rest[1, rows]) + 20.0 * got[k % 2, here]
            square = jnp.maximum(square, 0.25)
            new = root(square)
            new_r[rows] = new
            taken = (0.0003 * m) * (square * new - r * r * r)
            cond[rows] = taken + pltpu.roll(taken, 64, 1)
            return 0

        lax.fori_loop(0, per // 64, grow, 0, unroll=4)
        c = pltpu.make_async_copy(
            new_r.at[pl.ds(k * per, per)], parts_out.at[0, pl.ds(k * per, per)], sems.at[k]
        )
        c.start()
        outs.append(c)
    slot = lax.broadcasted_iota(jnp.int32, (SLOTS, LEV), 0)
    for n, d in enumerate((2, 3)):
        dst = ahead.at[n]
        fetch_rows(SLOTS, lambda s, d=d: places[0, 0, d, s], [(new_r, dst)])
        dst[...] = jnp.where(slot < tallies[0, 0, d], dst[...], 0.0)

    def clear(g, _):
        for k in range(LANES_ACC):
            acc[k, pl.ds(pl.multiple_of(g * 128, 128), 128)] = jnp.zeros((128, LEV), F32)
        return 0

    lax.fori_loop(0, ROWS // 128, clear, 0)
    scatter_rows(home, cond, acc, 0, FIRST)
    for c in outs + copies:
        c.wait()


def kernel_forward(ahead, rb, ra, yb, ya):
    steer((yb, ya), lambda n: n, ahead[0], ahead[1], lambda n: rb[n], lambda n: ra[n])


def kernel_deposit(home, cond, aq, at, acc_in, q_out, t_out, acc, qo, to, sems):
    scatter_rows(home, cond, acc, FIRST, NB)
    outs = []
    for j in range(CHUNKS):

        def gather(g, _, j=j):
            rows = pl.ds(pl.multiple_of(j * CROWS + g * 64, 64), 64)
            dep = acc[0, rows]
            for k in range(1, LANES_ACC):
                dep = dep + acc[k, rows]
            qo[rows] = aq[rows] - dep
            to[rows] = at[rows] + 2.5 * dep
            return 0

        lax.fori_loop(0, CROWS // 64, gather, 0)
        for n, (src, dst) in enumerate(((qo, q_out), (to, t_out))):
            rows = pl.ds(j * CROWS, CROWS)
            c = pltpu.make_async_copy(src.at[rows], dst.at[rows], sems.at[n, j])
            c.start()
            outs.append(c)
    for c in outs:
        c.wait()


def kernel_arrive(rb, ra, mb, ma, yrb, yra, ymb, yma, out, buf, sems):
    ox, oy = odd_x(), odd_y()
    copies = []
    for d, odd, one, two, n, skip in (
        (0, ox, (ra, ma), (rb, mb), 0, 2), (1, ox, (rb, mb), (ra, ma), 0, 2),
        *((NORTH[n], oy, (yra, yma), (yrb, ymb), n, 0) for n in range(3)),
        *((SOUTH[n], oy, (yrb, ymb), (yra, yma), n, 0) for n in range(3)),
    ):
        buf[d, 0] = jnp.where(odd, one[0][n], two[0][n])
        for p in range(2):
            k = skip + 2 * n + p
            buf[d, 1 + p] = jnp.where(odd, one[1][k], two[1][k])
        copies.append(pltpu.make_async_copy(buf.at[d], out.at[d], sems.at[d]))
        copies[-1].start()
    for c in copies:
        c.wait()


def vmem(*shape):
    return pltpu.VMEM(shape, F32)


def hbm(*shape):
    return pltpu.HBM(shape, F32)


def in_hbm(x):
    return pltpu.with_memory_space_constraint(x, pltpu.HBM)


def dma(*shape):
    return pltpu.SemaphoreType.DMA(shape)


def call(kernel, name, us, ins, outs, shapes, scratch, aliases=None, mib=24):
    return pl.pallas_call(
        kernel,
        in_specs=ins,
        out_specs=outs,
        out_shape=shapes,
        scratch_shapes=scratch,
        input_output_aliases=aliases or {},
        compiler_params=pltpu.CompilerParams(vmem_limit_bytes=mib << 20),
        cost_estimate=pl.CostEstimate(flops=0, bytes_accessed=int(us * 3.0e6), transcendentals=0),
        name=name,
    )


def swapped(value, axis, phase):
    count = lax.axis_size(axis)
    step = [1 if (i + phase) % 2 == 0 else -1 for i in range(count)]
    return lax.ppermute(value, axis, [(i, (i + step[i]) % count) for i in range(count)])


def body(q, t, we, wn, parts, home, places, tallies):
    parts = in_hbm(parts.transpose(1, 0, 2))
    q_h, t_h = in_hbm(q), in_hbm(t)
    flat = [in_hbm(x.reshape(ROWS, LEV)) for x in (q, t, we, wn)]
    places_h, tallies_h, home_h = in_hbm(places), in_hbm(tallies), in_hbm(home)
    places_s, tallies_s = pltpu.SMEM((1, 1, 8, SLOTS), jnp.int32), pltpu.SMEM((1, 1, 8), jnp.int32)
    cells, table_of, blocks = vmem(ROWS, LEV), vmem(2 * ROWS, LEV), vmem(NB, LEV)
    pairs, radii = vmem(6, SLOTS, LEV), vmem(3, SLOTS, LEV)
    sums = vmem(LANES_ACC, ROWS, LEV)
    xb, xa, yb, ya, rest = call(
        kernel_send, "send_edges", 1, [ANY] * 5, [VM] * 5,
        [vmem(8, CY, LEV)] * 2 + [vmem(2, CX, LEV)] * 2 + [vmem(2, NB, LEV)],
        [vmem(2, 2, CY, LEV), vmem(2, 2, CX, 8, LEV), places_s, tallies_s, dma(2, 2), dma(2, 2), dma(4)],
    )(q_h, t_h, places_h, tallies_h, parts)
    hxb = swapped(xb, "gx", 1)
    hxa = swapped(xa, "gx", 0)
    hyb = swapped(yb, "gy", 1)
    hya = swapped(ya, "gy", 0)
    aq, at, table, cw, cs, radius, leave_b, leave_a, along_y = call(
        kernel_advect, "advect", 6, [ANY] * 2 + [VM] + [ANY] * 5, [VM] * 9,
        [cells, cells, table_of, vmem(CY, LEV), vmem(CX, LEV), blocks, radii, radii,
         vmem(2, 2, SLOTS, LEV)],
        [cells] * 4 + [places_s, tallies_s, dma(4, CHUNKS), dma(3)],
    )(places_h, tallies_h, rest, *flat, parts)
    aq, at, table, rb, ra, ymb, yma = call(
        kernel_fix, "fix_edges", 1, [ANY] * 3 + [VM] * 14, [VM] * 7,
        [cells, cells, table_of, radii, radii, pairs, pairs],
        [vmem(SLOTS, LEV), places_s, tallies_s, pltpu.SMEM((NB,), jnp.int32), dma(3)],
        {14: 0, 15: 1, 16: 2},
    )(places_h, tallies_h, home_h, hxb, hxa, hyb, hya, cw, cs, leave_b, leave_a, xb, xa, along_y, aq, at, table)
    rb = swapped(rb, "gx", 1)
    ra = swapped(ra, "gx", 0)
    ymb = swapped(ymb, "gy", 1)
    yma = swapped(yma, "gy", 0)
    parts_out, cond, ahead, acc = call(
        kernel_grow, "grow", 6, [SM] * 3 + [VM] * 3, [ANY, VM, VM, VM],
        [hbm(3, NB, LEV), blocks, vmem(2, SLOTS, LEV), sums],
        [vmem(2, NB // CHUNKS, LEV), blocks, dma(CHUNKS), dma(2)],
    )(places, tallies, home, table, radius, rest)
    yb, ya = call(kernel_forward, "forward", 1, [VM] * 3, [VM] * 2, [radii, radii], [])(ahead, rb, ra)
    yrb = swapped(yb, "gy", 1)
    yra = swapped(ya, "gy", 0)
    q_out, t_out, _ = call(
        kernel_deposit, "deposit", 4, [SM] + [VM] * 4, [ANY, ANY, VM],
        [hbm(ROWS, LEV), hbm(ROWS, LEV), sums], [cells, cells, dma(2, CHUNKS)], {4: 2},
    )(home, cond, aq, at, acc)
    arrived = call(
        kernel_arrive, "arrive", 1, [VM] * 8, ANY, hbm(8, 3, SLOTS, LEV),
        [vmem(8, 3, SLOTS, LEV), dma(8)],
    )(rb, ra, hxb, hxa, yrb, yra, ymb, yma)
    incoming = arrived.transpose(0, 2, 1, 3)[None, None]
    shape = (CX, CY, LEV)
    return q_out.reshape(shape), t_out.reshape(shape), parts_out.transpose(1, 0, 2), incoming


def solution(mesh):
    cells = P("gx", "gy", None)
    blocks = P(("gx", "gy"), None, None)
    return jax.shard_map(
        body,
        mesh=mesh,
        in_specs=(cells, cells, cells, cells, blocks, P(("gx", "gy")),
                  P("gx", "gy", None, None), P("gx", "gy", None)),
        out_specs=(cells, cells, blocks, P("gx", "gy", None, None, None, None)),
        check_vma=False,
    )
```

```python
import math

import jax
import jax.numpy as jnp
from jax import lax
from jax.experimental import pallas as pl
from jax.experimental.pallas import tpu as pltpu
from jax.sharding import PartitionSpec as P

CX, CY, LEV = 32, 64, 128
ROWS = CX * CY
NB = 2048
SLOTS = 64
CHUNKS = 8
CROWS = ROWS // CHUNKS
LANES_ACC = 4
UNROLL = 8
FIRST = 1536
POWER = 17.27 * (273.15 - 35.86) * math.log2(math.e)
SHIFT = 17.27 * math.log2(math.e) + math.log2(3.8)
F32 = jnp.float32
ANY = pl.BlockSpec(memory_space=pltpu.HBM)
VM = pl.BlockSpec(memory_space=pltpu.VMEM)
SM = pl.BlockSpec(memory_space=pltpu.SMEM)


EAST, WEST, NORTH, SOUTH = (0, 4, 5), (1, 6, 7), (2, 4, 6), (3, 5, 7)


def supersat(q, t):
    return q * jnp.exp2(POWER / (t - 35.86) - SHIFT) - 1.0


def both_halves(s):
    low = lax.broadcasted_iota(jnp.int32, s.shape, 1) < 64
    turned = pltpu.roll(s, 64, 1)
    return jnp.where(low, s, turned), jnp.where(low, turned, s)


def root(x):
    return x * lax.rsqrt(x)


def growth_base(r, sol):
    inv = 1.0 / r
    return r * r + 20.0 * (sol * (inv * inv * inv) - 0.01 * inv)


def fetch_rows(count, place, pairs, step=64):
    def group(g, _):
        slots = [g * step + u for u in range(step)]
        rows = [place(s) for s in slots]
        values = [[src[pl.ds(row, 1)] for row in rows] for src, _ in pairs]
        for (_, dst), column in zip(pairs, values):
            for s, value in zip(slots, column):
                dst[pl.ds(s, 1)] = value
        return 0

    lax.fori_loop(0, count // step, group, 0)


def odd_x():
    return lax.rem(lax.axis_index("gx"), 2) == 1


def odd_y():
    return lax.rem(lax.axis_index("gy"), 2) == 1


def gx_sends(sends):
    ox = odd_x()
    for send, odd in zip(sends, (jnp.logical_not(ox), ox)):
        for n in range(3):
            yield send, n, jnp.where(odd, WEST[n], EAST[n])


def kernel_send(
    q_h, t_h, places_h, tallies_h, parts_h, xb, xa, yb, ya, rest,
    slabs, tiles, places, tallies, xsem, ysem, sems,
):
    copies = []
    for f, src in enumerate((q_h, t_h)):
        for side in range(2):
            copies.append(pltpu.make_async_copy(
                src.at[:, pl.ds((CY - 8) * side, 8)], tiles.at[f, side], ysem.at[f, side]))
            copies.append(pltpu.make_async_copy(
                src.at[(CX - 1) * side], slabs.at[f, side], xsem.at[f, side]))
    copies.append(pltpu.make_async_copy(places_h, places, sems.at[0]))
    copies.append(pltpu.make_async_copy(tallies_h, tallies, sems.at[1]))
    planes = [pltpu.make_async_copy(parts_h.at[1 + p], rest.at[p], sems.at[2 + p]) for p in range(2)]
    for c in copies + planes:
        c.start()
    for c in copies:
        c.wait()
    ox, oy = odd_x(), odd_y()
    for f in range(2):
        low, high = slabs[f, 0], slabs[f, 1]
        xa[f] = jnp.where(ox, low, high)
        xb[f] = jnp.where(ox, high, low)
        low, high = tiles[f, 0, :, 0, :], tiles[f, 1, :, 7, :]
        ya[f] = jnp.where(oy, low, high)
        yb[f] = jnp.where(oy, high, low)
    slot = lax.broadcasted_iota(jnp.int32, (SLOTS, LEV), 0)
    for p in range(2):
        planes[p].wait()
        for send, n, d in gx_sends((xb, xa)):
            if n == 0:
                continue
            dst = send.at[2 * n + p]
            fetch_rows(SLOTS, lambda s, d=d: places[0, 0, d, s], [(rest.at[p], dst)])
            dst[...] = jnp.where(slot < tallies[0, 0, d], dst[...], 0.0)


def stencil(fields, sems, outs):
    aq, at, table = outs
    per = CX // CHUNKS
    copies = {
        (f, k): pltpu.make_async_copy(
            src.at[pl.ds(k * CROWS, CROWS)], dst.at[pl.ds(k * CROWS, CROWS)], sems.at[f, k]
        )
        for k in range(CHUNKS)
        for f, (src, dst) in enumerate(fields)
    }
    for c in copies.values():
        c.start()
    (_, qv), (_, tv), (_, wev), (_, wnv) = fields
    yi = lax.broadcasted_iota(jnp.int32, (CY, LEV), 0)
    first, last = yi == 0, yi == CY - 1
    kn = jnp.where(last, 0.0, 0.1).astype(F32)

    def slab(x, _):
        r0 = pl.multiple_of(x * CY, CY)
        rw = pl.multiple_of(jnp.maximum(x - 1, 0) * CY, CY)
        re = pl.multiple_of(jnp.minimum(x + 1, CX - 1) * CY, CY)
        here = pl.ds(r0, CY)
        we, wn = wev[here], wnv[here]
        mid = 0.6 - we - wn
        kw = (we + 0.1) * jnp.where(x > 0, 1.0, 0.0)
        ks = jnp.where(first, 0.0, wn + 0.1)
        ke = jnp.where(x < CX - 1, 0.1, 0.0)

        def carried(v):
            f = v[here]
            return (
                mid * f
                + kw * v[pl.ds(rw, CY)]
                + ks * pltpu.roll(f, 1, 0)
                + ke * v[pl.ds(re, CY)]
                + kn * pltpu.roll(f, CY - 1, 0)
            )

        q, t = carried(qv), carried(tv)
        aq[here] = q
        at[here] = t
        even, odd = both_halves(supersat(q, t))
        table[pl.ds(2 * r0, CY, stride=2)] = even
        table[pl.ds(2 * r0 + 1, CY, stride=2)] = odd
        return 0

    waited = set()

    def wait(*keys):
        for key in keys:
            if key in copies and key not in waited:
                copies[key].wait()
                waited.add(key)

    for k in range(CHUNKS):
        wait(*[(f, j) for j in (k - 1, k, k + 1) for f in range(2)], (2, k), (3, k))
        lax.fori_loop(k * per, (k + 1) * per, slab, 0, unroll=4)


def kernel_advect(
    places_h, tallies_h, rest, q_h, t_h, we_h, wn_h, parts_h,
    aq, at, table, cw, cs, radius, leave_b, leave_a, straight_b, straight_a, along_y,
    qv, tv, wev, wnv, places, tallies, sems, psem,
):
    copies = [
        pltpu.make_async_copy(places_h, places, psem.at[0]),
        pltpu.make_async_copy(tallies_h, tallies, psem.at[2]),
        pltpu.make_async_copy(parts_h.at[0], radius, psem.at[1]),
    ]
    for c in copies:
        c.start()
    stencil(((q_h, qv), (t_h, tv), (we_h, wev), (wn_h, wnv)), sems, (aq, at, table))
    cw[...] = wev[0:CY] + 0.1
    cs[...] = wnv[pl.ds(0, CX, stride=CY)] + 0.1
    for c in copies:
        c.wait()
    for leave, n, d in gx_sends((leave_b, leave_a)):
        fetch_rows(SLOTS, lambda s, d=d: places[0, 0, d, s], [(radius, leave.at[n])])
    slot = lax.broadcasted_iota(jnp.int32, (SLOTS, LEV), 0)
    ox = odd_x()
    straight = (
        (straight_b, jnp.where(ox, EAST[0], WEST[0])), (straight_a, jnp.where(ox, WEST[0], EAST[0])),
        (along_y.at[0], NORTH[0]), (along_y.at[1], SOUTH[0]),
    )
    for pair, d in straight:
        for p in range(2):
            dst = pair.at[p]
            fetch_rows(SLOTS, lambda s, d=d: places[0, 0, d, s], [(rest.at[p], dst)])
            dst[...] = jnp.where(slot < tallies[0, 0, d], dst[...], 0.0)


def steer(sends, place, north, south, of_b, of_a):
    ox, oy = odd_x(), odd_y()
    for n in range(3):
        if n == 0:
            up, down = north, south
        else:
            one, two = (of_a, of_b) if n == 1 else (of_b, of_a)
            up = jnp.where(ox, one(1), two(1))
            down = jnp.where(ox, one(2), two(2))
        sends[0][place(n)] = jnp.where(oy, up, down)
        sends[1][place(n)] = jnp.where(oy, down, up)


def scatter_rows(home, cond, acc, start, stop):
    half = lax.broadcasted_iota(jnp.int32, (1, LEV), 1) // 64

    def scatter(g, _):
        b0 = g * LANES_ACC
        where = [home[b0 + k] for k in range(LANES_ACC)]
        rows = [pl.ds(c >> 1, 1) for c in where]
        sums = [
            acc[k, rows[k]] + jnp.where(half == (where[k] & 1), cond[pl.ds(b0 + k, 1)], 0.0)
            for k in range(LANES_ACC)
        ]
        for k in range(LANES_ACC):
            acc[k, rows[k]] = sums[k]
        return 0

    lax.fori_loop(start // LANES_ACC, stop // LANES_ACC, scatter, 0, unroll=UNROLL)


def kernel_fix(
    places_h, tallies_h, home_h, hxb, hxa, hyb, hya, cw, cs, leave_b, leave_a, straight_b, straight_a, xb, xa, along_y, aq_in, at_in, table_in,
    aq, at, table, send_b, send_a, rest_b, rest_a, got, places, tallies, home, sems,
):
    lists = ((places_h, places), (tallies_h, tallies), (home_h, home))
    copies = [pltpu.make_async_copy(a, b, sems.at[k]) for k, (a, b) in enumerate(lists)]
    for c in copies:
        c.start()
    ox, oy = odd_x(), odd_y()
    for f, a in ((0, aq), (1, at)):
        a[0:CY] += cw[...] * jnp.where(ox, hxa[f], hxb[f])
        a[ROWS - CY : ROWS] += 0.1 * jnp.where(ox, hxb[f], hxa[f])
        a[pl.ds(0, CX, stride=CY)] += cs[...] * jnp.where(oy, hya[f], hyb[f])
        a[pl.ds(CY - 1, CX, stride=CY)] += 0.1 * jnp.where(oy, hyb[f], hya[f])

    def refresh(rows, start, count, stride):
        even, odd = both_halves(supersat(aq[rows], at[rows]))
        table[pl.ds(2 * start, count, stride=2 * stride)] = even
        table[pl.ds(2 * start + 1, count, stride=2 * stride)] = odd

    refresh(pl.ds(0, CY), 0, CY, 1)
    refresh(pl.ds(ROWS - CY, CY), ROWS - CY, CY, 1)
    refresh(pl.ds(0, CX, stride=CY), 0, CX, CY)
    refresh(pl.ds(CY - 1, CX, stride=CY), CY - 1, CX, CY)
    for c in copies:
        c.wait()
    slot = lax.broadcasted_iota(jnp.int32, (SLOTS, LEV), 0)
    radii, rests, straight = (leave_b, leave_a), (xb, xa), (straight_b, straight_a)
    for k, (send, n, d) in enumerate(gx_sends((send_b, send_a))):
        fetch_rows(SLOTS, lambda s, d=d: home[places[0, 0, d, s]], [(table, got)])
        if n == 0:
            solute = straight[k // 3][1]
            send[3], send[4] = straight[k // 3][0], solute
        else:
            solute = rests[k // 3][2 * n + 1]
        square = growth_base(radii[k // 3][n], solute) + 20.0 * got[...]
        send[n] = jnp.where(slot < tallies[0, 0, d], root(jnp.maximum(square, 0.25)), 0.0)
    for p in range(2):
        steer(
            (rest_b, rest_a), lambda n, p=p: 2 * n + p, along_y[0, p], along_y[1, p],
            lambda n, p=p: hxb[2 * n + p], lambda n, p=p: hxa[2 * n + p],
        )


def kernel_grow(places, tallies, home, table, radius, rest, parts_out, cond, ahead, acc, got, new_r, sems, psem):
    copies = [pltpu.make_async_copy(rest.at[p], parts_out.at[1 + p], psem.at[p]) for p in range(2)]
    for c in copies:
        c.start()
    outs = []
    per = NB // CHUNKS
    for k in range(CHUNKS):
        fetch_rows(per, lambda s, k=k: home[k * per + s], [(table, got.at[k % 2])])

        def grow(g, _, k=k):
            here = pl.ds(pl.multiple_of(g * 64, 64), 64)
            rows = pl.ds(pl.multiple_of(k * per + g * 64, 64), 64)
            r, m = radius[rows], rest[0, rows]
            square = growth_base(r, rest[1, rows]) + 20.0 * got[k % 2, here]
            square = jnp.maximum(square, 0.25)
            new = root(square)
            new_r[rows] = new
            taken = (0.0003 * m) * (square * new - r * r * r)
            cond[rows] = taken + pltpu.roll(taken, 64, 1)
            return 0

        lax.fori_loop(0, per // 64, grow, 0, unroll=4)
        c = pltpu.make_async_copy(
            new_r.at[pl.ds(k * per, per)], parts_out.at[0, pl.ds(k * per, per)], sems.at[k]
        )
        c.start()
        outs.append(c)
    slot = lax.broadcasted_iota(jnp.int32, (SLOTS, LEV), 0)
    for n, d in enumerate((2, 3)):
        dst = ahead.at[n]
        fetch_rows(SLOTS, lambda s, d=d: places[0, 0, d, s], [(new_r, dst)])
        dst[...] = jnp.where(slot < tallies[0, 0, d], dst[...], 0.0)

    def clear(g, _):
        for k in range(LANES_ACC):
            acc[k, pl.ds(pl.multiple_of(g * 128, 128), 128)] = jnp.zeros((128, LEV), F32)
        return 0

    lax.fori_loop(0, ROWS // 128, clear, 0)
    scatter_rows(home, cond, acc, 0, FIRST)
    for c in outs + copies:
        c.wait()


def kernel_forward(ahead, rb, ra, yb, ya):
    steer((yb, ya), lambda n: n, ahead[0], ahead[1], lambda n: rb[n], lambda n: ra[n])


def kernel_deposit(home, cond, aq, at, acc_in, q_out, t_out, acc, qo, to, sems):
    scatter_rows(home, cond, acc, FIRST, NB)
    outs = []
    for j in range(CHUNKS):

        def gather(g, _, j=j):
            rows = pl.ds(pl.multiple_of(j * CROWS + g * 64, 64), 64)
            dep = acc[0, rows]
            for k in range(1, LANES_ACC):
                dep = dep + acc[k, rows]
            qo[rows] = aq[rows] - dep
            to[rows] = at[rows] + 2.5 * dep
            return 0

        lax.fori_loop(0, CROWS // 64, gather, 0)
        for n, (src, dst) in enumerate(((qo, q_out), (to, t_out))):
            rows = pl.ds(j * CROWS, CROWS)
            c = pltpu.make_async_copy(src.at[rows], dst.at[rows], sems.at[n, j])
            c.start()
            outs.append(c)
    for c in outs:
        c.wait()


def kernel_arrive(rb, ra, yrb, yra, ymb, yma, out, buf, sems):
    ox, oy = odd_x(), odd_y()
    copies = []
    for d, odd, one, two, n, skip in (
        (0, ox, (ra, ra), (rb, rb), 0, 3), (1, ox, (rb, rb), (ra, ra), 0, 3),
        *((NORTH[n], oy, (yra, yma), (yrb, ymb), n, 0) for n in range(3)),
        *((SOUTH[n], oy, (yrb, ymb), (yra, yma), n, 0) for n in range(3)),
    ):
        buf[d, 0] = jnp.where(odd, one[0][n], two[0][n])
        for p in range(2):
            k = skip + 2 * n + p
            buf[d, 1 + p] = jnp.where(odd, one[1][k], two[1][k])
        copies.append(pltpu.make_async_copy(buf.at[d], out.at[d], sems.at[d]))
        copies[-1].start()
    for c in copies:
        c.wait()


def vmem(*shape):
    return pltpu.VMEM(shape, F32)


def hbm(*shape):
    return pltpu.HBM(shape, F32)


def in_hbm(x):
    return pltpu.with_memory_space_constraint(x, pltpu.HBM)


def dma(*shape):
    return pltpu.SemaphoreType.DMA(shape)


def call(kernel, name, us, ins, outs, shapes, scratch, aliases=None, mib=24):
    return pl.pallas_call(
        kernel,
        in_specs=ins,
        out_specs=outs,
        out_shape=shapes,
        scratch_shapes=scratch,
        input_output_aliases=aliases or {},
        compiler_params=pltpu.CompilerParams(vmem_limit_bytes=mib << 20),
        cost_estimate=pl.CostEstimate(flops=0, bytes_accessed=int(us * 3.0e6), transcendentals=0),
        name=name,
    )


def swapped(value, axis, phase):
    count = lax.axis_size(axis)
    step = [1 if (i + phase) % 2 == 0 else -1 for i in range(count)]
    return lax.ppermute(value, axis, [(i, (i + step[i]) % count) for i in range(count)])


def body(q, t, we, wn, parts, home, places, tallies):
    parts = in_hbm(parts.transpose(1, 0, 2))
    q_h, t_h = in_hbm(q), in_hbm(t)
    flat = [in_hbm(x.reshape(ROWS, LEV)) for x in (q, t, we, wn)]
    places_h, tallies_h, home_h = in_hbm(places), in_hbm(tallies), in_hbm(home)
    places_s, tallies_s = pltpu.SMEM((1, 1, 8, SLOTS), jnp.int32), pltpu.SMEM((1, 1, 8), jnp.int32)
    cells, table_of, blocks = vmem(ROWS, LEV), vmem(2 * ROWS, LEV), vmem(NB, LEV)
    pairs, radii = vmem(6, SLOTS, LEV), vmem(3, SLOTS, LEV)
    sums = vmem(LANES_ACC, ROWS, LEV)
    xb, xa, yb, ya, rest = call(
        kernel_send, "send_edges", 1, [ANY] * 5, [VM] * 5,
        [vmem(6, CY, LEV)] * 2 + [vmem(2, CX, LEV)] * 2 + [vmem(2, NB, LEV)],
        [vmem(2, 2, CY, LEV), vmem(2, 2, CX, 8, LEV), places_s, tallies_s, dma(2, 2), dma(2, 2), dma(4)],
    )(q_h, t_h, places_h, tallies_h, parts)
    hxb = swapped(xb, "gx", 1)
    hxa = swapped(xa, "gx", 0)
    hyb = swapped(yb, "gy", 1)
    hya = swapped(ya, "gy", 0)
    aq, at, table, cw, cs, radius, leave_b, leave_a, straight_b, straight_a, along_y = call(
        kernel_advect, "advect", 6, [ANY] * 2 + [VM] + [ANY] * 5, [VM] * 11,
        [cells, cells, table_of, vmem(CY, LEV), vmem(CX, LEV), blocks, radii, radii,
         vmem(2, SLOTS, LEV), vmem(2, SLOTS, LEV), vmem(2, 2, SLOTS, LEV)],
        [cells] * 4 + [places_s, tallies_s, dma(4, CHUNKS), dma(3)],
    )(places_h, tallies_h, rest, *flat, parts)
    aq, at, table, rb, ra, ymb, yma = call(
        kernel_fix, "fix_edges", 1, [ANY] * 3 + [VM] * 16, [VM] * 7,
        [cells, cells, table_of, vmem(5, SLOTS, LEV), vmem(5, SLOTS, LEV), pairs, pairs],
        [vmem(SLOTS, LEV), places_s, tallies_s, pltpu.SMEM((NB,), jnp.int32), dma(3)],
        {16: 0, 17: 1, 18: 2},
    )(places_h, tallies_h, home_h, hxb, hxa, hyb, hya, cw, cs, leave_b, leave_a, straight_b, straight_a,
      xb, xa, along_y, aq, at, table)
    rb = swapped(rb, "gx", 1)
    ra = swapped(ra, "gx", 0)
    ymb = swapped(ymb, "gy", 1)
    yma = swapped(yma, "gy", 0)
    parts_out, cond, ahead, acc = call(
        kernel_grow, "grow", 6, [SM] * 3 + [VM] * 3, [ANY, VM, VM, VM],
        [hbm(3, NB, LEV), blocks, vmem(2, SLOTS, LEV), sums],
        [vmem(2, NB // CHUNKS, LEV), blocks, dma(CHUNKS), dma(2)],
    )(places, tallies, home, table, radius, rest)
    yb, ya = call(kernel_forward, "forward", 1, [VM] * 3, [VM] * 2, [radii, radii], [])(ahead, rb, ra)
    yrb = swapped(yb, "gy", 1)
    yra = swapped(ya, "gy", 0)
    q_out, t_out, _ = call(
        kernel_deposit, "deposit", 4, [SM] + [VM] * 4, [ANY, ANY, VM],
        [hbm(ROWS, LEV), hbm(ROWS, LEV), sums], [cells, cells, dma(2, CHUNKS)], {4: 2},
    )(home, cond, aq, at, acc)
    arrived = call(
        kernel_arrive, "arrive", 1, [VM] * 6, ANY, hbm(8, 3, SLOTS, LEV),
        [vmem(8, 3, SLOTS, LEV), dma(8)],
    )(rb, ra, yrb, yra, ymb, yma)
    incoming = arrived.transpose(0, 2, 1, 3)[None, None]
    shape = (CX, CY, LEV)
    return q_out.reshape(shape), t_out.reshape(shape), parts_out.transpose(1, 0, 2), incoming


def solution(mesh):
    cells = P("gx", "gy", None)
    blocks = P(("gx", "gy"), None, None)
    return jax.shard_map(
        body,
        mesh=mesh,
        in_specs=(cells, cells, cells, cells, blocks, P(("gx", "gy")),
                  P("gx", "gy", None, None), P("gx", "gy", None)),
        out_specs=(cells, cells, blocks, P("gx", "gy", None, None, None, None)),
        check_vma=False,
    )
```

```python
import math

import jax
import jax.numpy as jnp
from jax import lax
from jax.experimental import pallas as pl
from jax.experimental.pallas import tpu as pltpu
from jax.sharding import PartitionSpec as P

CX, CY, LEV = 32, 64, 128
ROWS = CX * CY
NB = 2048
SLOTS = 64
CHUNKS = 8
CROWS = ROWS // CHUNKS
LANES_ACC = 4
UNROLL = 8
POWER = 17.27 * (273.15 - 35.86) * math.log2(math.e)
SHIFT = 17.27 * math.log2(math.e) + math.log2(3.8)
F32 = jnp.float32
ANY = pl.BlockSpec(memory_space=pltpu.HBM)
VM = pl.BlockSpec(memory_space=pltpu.VMEM)
SM = pl.BlockSpec(memory_space=pltpu.SMEM)


EAST, WEST, NORTH, SOUTH = (0, 4, 5), (1, 6, 7), (2, 4, 6), (3, 5, 7)


def supersat(q, t):
    return q * jnp.exp2(POWER / (t - 35.86) - SHIFT) - 1.0


def both_halves(s):
    low = lax.broadcasted_iota(jnp.int32, s.shape, 1) < 64
    turned = pltpu.roll(s, 64, 1)
    return jnp.where(low, s, turned), jnp.where(low, turned, s)


def root(x):
    return x * lax.rsqrt(x)


def growth_base(r, sol):
    inv = 1.0 / r
    return r * r + 20.0 * (sol * (inv * inv * inv) - 0.01 * inv)


def fetch_rows(count, place, pairs, step=64):
    def group(g, _):
        slots = [g * step + u for u in range(step)]
        rows = [place(s) for s in slots]
        values = [[src[pl.ds(row, 1)] for row in rows] for src, _ in pairs]
        for (_, dst), column in zip(pairs, values):
            for s, value in zip(slots, column):
                dst[pl.ds(s, 1)] = value
        return 0

    lax.fori_loop(0, count // step, group, 0)


def odd_x():
    return lax.rem(lax.axis_index("gx"), 2) == 1


def odd_y():
    return lax.rem(lax.axis_index("gy"), 2) == 1


def gx_sends(sends):
    ox = odd_x()
    for send, odd in zip(sends, (jnp.logical_not(ox), ox)):
        for n in range(3):
            yield send, n, jnp.where(odd, WEST[n], EAST[n])


def kernel_send(
    q_h, t_h, places_h, tallies_h, parts_h, xb, xa, yb, ya, rest,
    slabs, tiles, places, tallies, xsem, ysem, sems,
):
    copies = []
    for f, src in enumerate((q_h, t_h)):
        for side in range(2):
            copies.append(pltpu.make_async_copy(
                src.at[:, pl.ds((CY - 8) * side, 8)], tiles.at[f, side], ysem.at[f, side]))
            copies.append(pltpu.make_async_copy(
                src.at[(CX - 1) * side], slabs.at[f, side], xsem.at[f, side]))
    copies.append(pltpu.make_async_copy(places_h, places, sems.at[0]))
    copies.append(pltpu.make_async_copy(tallies_h, tallies, sems.at[1]))
    planes = [pltpu.make_async_copy(parts_h.at[1 + p], rest.at[p], sems.at[2 + p]) for p in range(2)]
    for c in copies + planes:
        c.start()
    for c in copies:
        c.wait()
    ox, oy = odd_x(), odd_y()
    for f in range(2):
        low, high = slabs[f, 0], slabs[f, 1]
        xa[f] = jnp.where(ox, low, high)
        xb[f] = jnp.where(ox, high, low)
        low, high = tiles[f, 0, :, 0, :], tiles[f, 1, :, 7, :]
        ya[f] = jnp.where(oy, low, high)
        yb[f] = jnp.where(oy, high, low)
    slot = lax.broadcasted_iota(jnp.int32, (SLOTS, LEV), 0)
    for p in range(2):
        planes[p].wait()
        for send, n, d in gx_sends((xb, xa)):
            if n == 0:
                continue
            dst = send.at[2 * n + p]
            fetch_rows(SLOTS, lambda s, d=d: places[0, 0, d, s], [(rest.at[p], dst)])
            dst[...] = jnp.where(slot < tallies[0, 0, d], dst[...], 0.0)


def stencil(fields, sems, outs):
    aq, at, table = outs
    per = CX // CHUNKS
    copies = {
        (f, k): pltpu.make_async_copy(
            src.at[pl.ds(k * CROWS, CROWS)], dst.at[pl.ds(k * CROWS, CROWS)], sems.at[f, k]
        )
        for k in range(CHUNKS)
        for f, (src, dst) in enumerate(fields)
    }
    for c in copies.values():
        c.start()
    (_, qv), (_, tv), (_, wev), (_, wnv) = fields
    yi = lax.broadcasted_iota(jnp.int32, (CY, LEV), 0)
    first, last = yi == 0, yi == CY - 1
    kn = jnp.where(last, 0.0, 0.1).astype(F32)

    def slab(x, _):
        r0 = pl.multiple_of(x * CY, CY)
        rw = pl.multiple_of(jnp.maximum(x - 1, 0) * CY, CY)
        re = pl.multiple_of(jnp.minimum(x + 1, CX - 1) * CY, CY)
        here = pl.ds(r0, CY)
        we, wn = wev[here], wnv[here]
        mid = 0.6 - we - wn
        kw = (we + 0.1) * jnp.where(x > 0, 1.0, 0.0)
        ks = jnp.where(first, 0.0, wn + 0.1)
        ke = jnp.where(x < CX - 1, 0.1, 0.0)

        def carried(v):
            f = v[here]
            return (
                mid * f
                + kw * v[pl.ds(rw, CY)]
                + ks * pltpu.roll(f, 1, 0)
                + ke * v[pl.ds(re, CY)]
                + kn * pltpu.roll(f, CY - 1, 0)
            )

        q, t = carried(qv), carried(tv)
        aq[here] = q
        at[here] = t
        even, odd = both_halves(supersat(q, t))
        table[pl.ds(2 * r0, CY, stride=2)] = even
        table[pl.ds(2 * r0 + 1, CY, stride=2)] = odd
        return 0

    waited = set()

    def wait(*keys):
        for key in keys:
            if key in copies and key not in waited:
                copies[key].wait()
                waited.add(key)

    for k in range(CHUNKS):
        wait(*[(f, j) for j in (k - 1, k, k + 1) for f in range(2)], (2, k), (3, k))
        lax.fori_loop(k * per, (k + 1) * per, slab, 0, unroll=4)


def kernel_advect(
    places_h, tallies_h, rest, q_h, t_h, we_h, wn_h, parts_h,
    aq, at, table, cw, cs, radius, base, acc, leave_b, leave_a, straight_b, straight_a, along_y,
    qv, tv, wev, wnv, places, tallies, sems, psem,
):
    copies = [
        pltpu.make_async_copy(places_h, places, psem.at[0]),
        pltpu.make_async_copy(tallies_h, tallies, psem.at[2]),
        pltpu.make_async_copy(parts_h.at[0], radius, psem.at[1]),
    ]
    for c in copies:
        c.start()
    stencil(((q_h, qv), (t_h, tv), (we_h, wev), (wn_h, wnv)), sems, (aq, at, table))
    cw[...] = wev[0:CY] + 0.1
    cs[...] = wnv[pl.ds(0, CX, stride=CY)] + 0.1
    for c in copies:
        c.wait()

    def prepare(g, _):
        rows = pl.ds(pl.multiple_of(g * 64, 64), 64)
        base[rows] = growth_base(radius[rows], rest[1, rows])
        for k in range(LANES_ACC):
            acc[k, rows] = jnp.zeros((64, LEV), F32)
        return 0

    lax.fori_loop(0, NB // 64, prepare, 0, unroll=2)
    for leave, n, d in gx_sends((leave_b, leave_a)):
        fetch_rows(SLOTS, lambda s, d=d: places[0, 0, d, s], [(base, leave.at[n])])
    slot = lax.broadcasted_iota(jnp.int32, (SLOTS, LEV), 0)
    ox = odd_x()
    straight = (
        (straight_b, jnp.where(ox, EAST[0], WEST[0])), (straight_a, jnp.where(ox, WEST[0], EAST[0])),
        (along_y.at[0], NORTH[0]), (along_y.at[1], SOUTH[0]),
    )
    for pair, d in straight:
        for p in range(2):
            dst = pair.at[p]
            fetch_rows(SLOTS, lambda s, d=d: places[0, 0, d, s], [(rest.at[p], dst)])
            dst[...] = jnp.where(slot < tallies[0, 0, d], dst[...], 0.0)


def steer(sends, place, north, south, of_b, of_a):
    ox, oy = odd_x(), odd_y()
    for n in range(3):
        if n == 0:
            up, down = north, south
        else:
            one, two = (of_a, of_b) if n == 1 else (of_b, of_a)
            up = jnp.where(ox, one(1), two(1))
            down = jnp.where(ox, one(2), two(2))
        sends[0][place(n)] = jnp.where(oy, up, down)
        sends[1][place(n)] = jnp.where(oy, down, up)


def scatter_rows(home, cond, acc, start, stop):
    half = lax.broadcasted_iota(jnp.int32, (1, LEV), 1) // 64

    def scatter(g, _):
        b0 = g * LANES_ACC
        where = [home[b0 + k] for k in range(LANES_ACC)]
        rows = [pl.ds(c >> 1, 1) for c in where]
        sums = [
            acc[k, rows[k]] + jnp.where(half == (where[k] & 1), cond[pl.ds(b0 + k, 1)], 0.0)
            for k in range(LANES_ACC)
        ]
        for k in range(LANES_ACC):
            acc[k, rows[k]] = sums[k]
        return 0

    lax.fori_loop(start // LANES_ACC, stop // LANES_ACC, scatter, 0, unroll=UNROLL)


def kernel_fix(
    places_h, tallies_h, home_h, hxb, hxa, hyb, hya, cw, cs, leave_b, leave_a, straight_b, straight_a, along_y, aq_in, at_in, table_in,
    aq, at, table, send_b, send_a, rest_b, rest_a, got, places, tallies, home, sems,
):
    lists = ((places_h, places), (tallies_h, tallies), (home_h, home))
    copies = [pltpu.make_async_copy(a, b, sems.at[k]) for k, (a, b) in enumerate(lists)]
    for c in copies:
        c.start()
    ox, oy = odd_x(), odd_y()
    for f, a in ((0, aq), (1, at)):
        a[0:CY] += cw[...] * jnp.where(ox, hxa[f], hxb[f])
        a[ROWS - CY : ROWS] += 0.1 * jnp.where(ox, hxb[f], hxa[f])
        a[pl.ds(0, CX, stride=CY)] += cs[...] * jnp.where(oy, hya[f], hyb[f])
        a[pl.ds(CY - 1, CX, stride=CY)] += 0.1 * jnp.where(oy, hyb[f], hya[f])

    def refresh(rows, start, count, stride):
        even, odd = both_halves(supersat(aq[rows], at[rows]))
        table[pl.ds(2 * start, count, stride=2 * stride)] = even
        table[pl.ds(2 * start + 1, count, stride=2 * stride)] = odd

    refresh(pl.ds(0, CY), 0, CY, 1)
    refresh(pl.ds(ROWS - CY, CY), ROWS - CY, CY, 1)
    refresh(pl.ds(0, CX, stride=CY), 0, CX, CY)
    refresh(pl.ds(CY - 1, CX, stride=CY), CY - 1, CX, CY)
    for c in copies:
        c.wait()
    slot = lax.broadcasted_iota(jnp.int32, (SLOTS, LEV), 0)
    bases, straight = (leave_b, leave_a), (straight_b, straight_a)
    for k, (send, n, d) in enumerate(gx_sends((send_b, send_a))):
        fetch_rows(SLOTS, lambda s, d=d: home[places[0, 0, d, s]], [(table, got)])
        if n == 0:
            send[3], send[4] = straight[k // 3][0], straight[k // 3][1]
        square = bases[k // 3][n] + 20.0 * got[...]
        send[n] = jnp.where(slot < tallies[0, 0, d], root(jnp.maximum(square, 0.25)), 0.0)
    for p in range(2):
        steer(
            (rest_b, rest_a), lambda n, p=p: 2 * n + p, along_y[0, p], along_y[1, p],
            lambda n, p=p: hxb[2 * n + p], lambda n, p=p: hxa[2 * n + p],
        )


def kernel_grow(places, tallies, home, table, radius, rest, base, acc_in, parts_out, ahead, acc, cond, got, new_r, sems, psem):
    copies = [pltpu.make_async_copy(rest.at[p], parts_out.at[1 + p], psem.at[p]) for p in range(2)]
    for c in copies:
        c.start()
    outs = []
    per = NB // CHUNKS
    for k in range(CHUNKS):
        fetch_rows(per, lambda s, k=k: home[k * per + s], [(table, got.at[k % 2])])

        def grow(g, _, k=k):
            here = pl.ds(pl.multiple_of(g * 64, 64), 64)
            rows = pl.ds(pl.multiple_of(k * per + g * 64, 64), 64)
            r, m = radius[rows], rest[0, rows]
            square = base[rows] + 20.0 * got[k % 2, here]
            square = jnp.maximum(square, 0.25)
            new = root(square)
            new_r[rows] = new
            taken = (0.0003 * m) * (square * new - r * r * r)
            cond[rows] = taken + pltpu.roll(taken, 64, 1)
            return 0

        lax.fori_loop(0, per // 64, grow, 0, unroll=4)
        c = pltpu.make_async_copy(
            new_r.at[pl.ds(k * per, per)], parts_out.at[0, pl.ds(k * per, per)], sems.at[k]
        )
        c.start()
        outs.append(c)
    slot = lax.broadcasted_iota(jnp.int32, (SLOTS, LEV), 0)
    for n, d in enumerate((2, 3)):
        dst = ahead.at[n]
        fetch_rows(SLOTS, lambda s, d=d: places[0, 0, d, s], [(new_r, dst)])
        dst[...] = jnp.where(slot < tallies[0, 0, d], dst[...], 0.0)
    scatter_rows(home, cond, acc, 0, NB)
    for c in outs + copies:
        c.wait()


def kernel_forward(ahead, ra, rb, yb, ya):
    steer((yb, ya), lambda n: n, ahead[0], ahead[1], lambda n: rb[n], lambda n: ra[n])


def kernel_deposit(aq, at, acc, q_out, t_out, qo, to, sems):
    outs = []
    for j in range(CHUNKS):

        def gather(g, _, j=j):
            rows = pl.ds(pl.multiple_of(j * CROWS + g * 64, 64), 64)
            dep = acc[0, rows]
            for k in range(1, LANES_ACC):
                dep = dep + acc[k, rows]
            qo[rows] = aq[rows] - dep
            to[rows] = at[rows] + 2.5 * dep
            return 0

        lax.fori_loop(0, CROWS // 64, gather, 0)
        for n, (src, dst) in enumerate(((qo, q_out), (to, t_out))):
            rows = pl.ds(j * CROWS, CROWS)
            c = pltpu.make_async_copy(src.at[rows], dst.at[rows], sems.at[n, j])
            c.start()
            outs.append(c)
    for c in outs:
        c.wait()


def kernel_arrive(ra, rb, yrb, yra, ymb, yma, out, buf, sems):
    ox, oy = odd_x(), odd_y()
    copies = []
    for d, odd, one, two, n, skip in (
        (0, ox, (ra, ra), (rb, rb), 0, 3), (1, ox, (rb, rb), (ra, ra), 0, 3),
        *((NORTH[n], oy, (yra, yma), (yrb, ymb), n, 0) for n in range(3)),
        *((SOUTH[n], oy, (yrb, ymb), (yra, yma), n, 0) for n in range(3)),
    ):
        buf[d, 0] = jnp.where(odd, one[0][n], two[0][n])
        for p in range(2):
            k = skip + 2 * n + p
            buf[d, 1 + p] = jnp.where(odd, one[1][k], two[1][k])
        copies.append(pltpu.make_async_copy(buf.at[d], out.at[d], sems.at[d]))
        copies[-1].start()
    for c in copies:
        c.wait()


def vmem(*shape):
    return pltpu.VMEM(shape, F32)


def hbm(*shape):
    return pltpu.HBM(shape, F32)


def in_hbm(x):
    return pltpu.with_memory_space_constraint(x, pltpu.HBM)


def dma(*shape):
    return pltpu.SemaphoreType.DMA(shape)


def call(kernel, name, us, ins, outs, shapes, scratch, aliases=None, mib=24):
    return pl.pallas_call(
        kernel,
        in_specs=ins,
        out_specs=outs,
        out_shape=shapes,
        scratch_shapes=scratch,
        input_output_aliases=aliases or {},
        compiler_params=pltpu.CompilerParams(vmem_limit_bytes=mib << 20),
        cost_estimate=pl.CostEstimate(flops=0, bytes_accessed=int(us * 3.0e6), transcendentals=0),
        name=name,
    )


def swapped(value, axis, phase):
    count = lax.axis_size(axis)
    step = [1 if (i + phase) % 2 == 0 else -1 for i in range(count)]
    return lax.ppermute(value, axis, [(i, (i + step[i]) % count) for i in range(count)])


def body(q, t, we, wn, parts, home, places, tallies):
    parts = in_hbm(parts.transpose(1, 0, 2))
    q_h, t_h = in_hbm(q), in_hbm(t)
    flat = [in_hbm(x.reshape(ROWS, LEV)) for x in (q, t, we, wn)]
    places_h, tallies_h, home_h = in_hbm(places), in_hbm(tallies), in_hbm(home)
    places_s, tallies_s = pltpu.SMEM((1, 1, 8, SLOTS), jnp.int32), pltpu.SMEM((1, 1, 8), jnp.int32)
    cells, table_of, blocks = vmem(ROWS, LEV), vmem(2 * ROWS, LEV), vmem(NB, LEV)
    pairs, radii = vmem(6, SLOTS, LEV), vmem(3, SLOTS, LEV)
    sums = vmem(LANES_ACC, ROWS, LEV)
    xb, xa, yb, ya, rest = call(
        kernel_send, "send_edges", 1, [ANY] * 5, [VM] * 5,
        [vmem(6, CY, LEV)] * 2 + [vmem(2, CX, LEV)] * 2 + [vmem(2, NB, LEV)],
        [vmem(2, 2, CY, LEV), vmem(2, 2, CX, 8, LEV), places_s, tallies_s, dma(2, 2), dma(2, 2), dma(4)],
    )(q_h, t_h, places_h, tallies_h, parts)
    hxb = swapped(xb, "gx", 1)
    hxa = swapped(xa, "gx", 0)
    hyb = swapped(yb, "gy", 1)
    hya = swapped(ya, "gy", 0)
    aq, at, table, cw, cs, radius, base, acc, leave_b, leave_a, straight_b, straight_a, along_y = call(
        kernel_advect, "advect", 6, [ANY] * 2 + [VM] + [ANY] * 5, [VM] * 13,
        [cells, cells, table_of, vmem(CY, LEV), vmem(CX, LEV), blocks, blocks, sums, radii, radii,
         vmem(2, SLOTS, LEV), vmem(2, SLOTS, LEV), vmem(2, 2, SLOTS, LEV)],
        [cells] * 4 + [places_s, tallies_s, dma(4, CHUNKS), dma(3)],
    )(places_h, tallies_h, rest, *flat, parts)
    aq, at, table, rb, ra, ymb, yma = call(
        kernel_fix, "fix_edges", 1, [ANY] * 3 + [VM] * 14, [VM] * 7,
        [cells, cells, table_of, vmem(5, SLOTS, LEV), vmem(5, SLOTS, LEV), pairs, pairs],
        [vmem(SLOTS, LEV), places_s, tallies_s, pltpu.SMEM((NB,), jnp.int32), dma(3)],
        {14: 0, 15: 1, 16: 2},
    )(places_h, tallies_h, home_h, hxb, hxa, hyb, hya, cw, cs, leave_b, leave_a, straight_b, straight_a, along_y,
      aq, at, table)
    rb = swapped(rb, "gx", 1)
    ra = swapped(ra, "gx", 0)
    ymb = swapped(ymb, "gy", 1)
    yma = swapped(yma, "gy", 0)
    parts_out, ahead, acc = call(
        kernel_grow, "grow", 6, [SM] * 3 + [VM] * 5, [ANY, VM, VM],
        [hbm(3, NB, LEV), vmem(2, SLOTS, LEV), sums],
        [blocks, vmem(2, NB // CHUNKS, LEV), blocks, dma(CHUNKS), dma(2)], {7: 2},
    )(places, tallies, home, table, radius, rest, base, acc)
    yb, ya = call(kernel_forward, "forward", 1, [VM] * 3, [VM] * 2, [radii, radii], [])(ahead, ra, rb)
    yrb = swapped(yb, "gy", 1)
    yra = swapped(ya, "gy", 0)
    q_out, t_out = call(
        kernel_deposit, "deposit", 4, [VM] * 3, [ANY, ANY],
        [hbm(ROWS, LEV), hbm(ROWS, LEV)], [cells, cells, dma(2, CHUNKS)],
    )(aq, at, acc)
    arrived = call(
        kernel_arrive, "arrive", 1, [VM] * 6, ANY, hbm(8, 3, SLOTS, LEV),
        [vmem(8, 3, SLOTS, LEV), dma(8)],
    )(ra, rb, yrb, yra, ymb, yma)
    incoming = arrived.transpose(0, 2, 1, 3)[None, None]
    shape = (CX, CY, LEV)
    return q_out.reshape(shape), t_out.reshape(shape), parts_out.transpose(1, 0, 2), incoming


def solution(mesh):
    cells = P("gx", "gy", None)
    blocks = P(("gx", "gy"), None, None)
    return jax.shard_map(
        body,
        mesh=mesh,
        in_specs=(cells, cells, cells, cells, blocks, P(("gx", "gy")),
                  P("gx", "gy", None, None), P("gx", "gy", None)),
        out_specs=(cells, cells, blocks, P("gx", "gy", None, None, None, None)),
        check_vma=False,
    )
```

```python
import math

import jax
import jax.numpy as jnp
from jax import lax
from jax.experimental import pallas as pl
from jax.experimental.pallas import tpu as pltpu
from jax.sharding import PartitionSpec as P

CX, CY, LEV = 32, 64, 128
ROWS = CX * CY
NB = 2048
SLOTS = 64
CHUNKS = 8
CROWS = ROWS // CHUNKS
LANES_ACC = 8
UNROLL = 4
POWER = 17.27 * (273.15 - 35.86) * math.log2(math.e)
SHIFT = 17.27 * math.log2(math.e) + math.log2(3.8)
F32 = jnp.float32
ANY = pl.BlockSpec(memory_space=pltpu.HBM)
VM = pl.BlockSpec(memory_space=pltpu.VMEM)
SM = pl.BlockSpec(memory_space=pltpu.SMEM)


EAST, WEST, NORTH, SOUTH = (0, 4, 5), (1, 6, 7), (2, 4, 6), (3, 5, 7)


def supersat(q, t):
    return q * jnp.exp2(POWER / (t - 35.86) - SHIFT) - 1.0


def both_halves(s):
    low = lax.broadcasted_iota(jnp.int32, s.shape, 1) < 64
    turned = pltpu.roll(s, 64, 1)
    return jnp.where(low, s, turned), jnp.where(low, turned, s)


def root(x):
    return x * lax.rsqrt(x)


def growth_base(r, sol):
    inv = 1.0 / r
    return r * r + 20.0 * (sol * (inv * inv * inv) - 0.01 * inv)


def fetch_rows(count, place, pairs, step=64):
    def group(g, _):
        slots = [g * step + u for u in range(step)]
        rows = [place(s) for s in slots]
        values = [[src[pl.ds(row, 1)] for row in rows] for src, _ in pairs]
        for (_, dst), column in zip(pairs, values):
            for s, value in zip(slots, column):
                dst[pl.ds(s, 1)] = value
        return 0

    lax.fori_loop(0, count // step, group, 0)


def odd_x():
    return lax.rem(lax.axis_index("gx"), 2) == 1


def odd_y():
    return lax.rem(lax.axis_index("gy"), 2) == 1


def gx_sends(sends):
    ox = odd_x()
    for send, odd in zip(sends, (jnp.logical_not(ox), ox)):
        for n in range(3):
            yield send, n, jnp.where(odd, WEST[n], EAST[n])


def kernel_send(
    q_h, t_h, places_h, tallies_h, parts_h, xb, xa, yb, ya, rest,
    slabs, tiles, places, tallies, xsem, ysem, sems,
):
    copies = []
    for f, src in enumerate((q_h, t_h)):
        for side in range(2):
            copies.append(pltpu.make_async_copy(
                src.at[:, pl.ds((CY - 8) * side, 8)], tiles.at[f, side], ysem.at[f, side]))
            copies.append(pltpu.make_async_copy(
                src.at[(CX - 1) * side], slabs.at[f, side], xsem.at[f, side]))
    copies.append(pltpu.make_async_copy(places_h, places, sems.at[0]))
    copies.append(pltpu.make_async_copy(tallies_h, tallies, sems.at[1]))
    planes = [pltpu.make_async_copy(parts_h.at[1 + p], rest.at[p], sems.at[2 + p]) for p in range(2)]
    for c in copies + planes:
        c.start()
    for c in copies:
        c.wait()
    ox, oy = odd_x(), odd_y()
    for f in range(2):
        low, high = slabs[f, 0], slabs[f, 1]
        xa[f] = jnp.where(ox, low, high)
        xb[f] = jnp.where(ox, high, low)
        low, high = tiles[f, 0, :, 0, :], tiles[f, 1, :, 7, :]
        ya[f] = jnp.where(oy, low, high)
        yb[f] = jnp.where(oy, high, low)
    slot = lax.broadcasted_iota(jnp.int32, (SLOTS, LEV), 0)
    for p in range(2):
        planes[p].wait()
        for send, n, d in gx_sends((xb, xa)):
            if n == 0:
                continue
            dst = send.at[2 * n + p]
            fetch_rows(SLOTS, lambda s, d=d: places[0, 0, d, s], [(rest.at[p], dst)])
            dst[...] = jnp.where(slot < tallies[0, 0, d], dst[...], 0.0)


def stencil(fields, sems, outs):
    aq, at, table = outs
    per = CX // CHUNKS
    copies = {
        (f, k): pltpu.make_async_copy(
            src.at[pl.ds(k * CROWS, CROWS)], dst.at[pl.ds(k * CROWS, CROWS)], sems.at[f, k]
        )
        for k in range(CHUNKS)
        for f, (src, dst) in enumerate(fields)
    }
    for c in copies.values():
        c.start()
    (_, qv), (_, tv), (_, wev), (_, wnv) = fields
    yi = lax.broadcasted_iota(jnp.int32, (CY, LEV), 0)
    first, last = yi == 0, yi == CY - 1
    kn = jnp.where(last, 0.0, 0.1).astype(F32)

    def slab(x, _):
        r0 = pl.multiple_of(x * CY, CY)
        rw = pl.multiple_of(jnp.maximum(x - 1, 0) * CY, CY)
        re = pl.multiple_of(jnp.minimum(x + 1, CX - 1) * CY, CY)
        here = pl.ds(r0, CY)
        we, wn = wev[here], wnv[here]
        mid = 0.6 - we - wn
        kw = (we + 0.1) * jnp.where(x > 0, 1.0, 0.0)
        ks = jnp.where(first, 0.0, wn + 0.1)
        ke = jnp.where(x < CX - 1, 0.1, 0.0)

        def carried(v):
            f = v[here]
            return (
                mid * f
                + kw * v[pl.ds(rw, CY)]
                + ks * pltpu.roll(f, 1, 0)
                + ke * v[pl.ds(re, CY)]
                + kn * pltpu.roll(f, CY - 1, 0)
            )

        q, t = carried(qv), carried(tv)
        aq[here] = q
        at[here] = t
        even, odd = both_halves(supersat(q, t))
        table[pl.ds(2 * r0, CY, stride=2)] = even
        table[pl.ds(2 * r0 + 1, CY, stride=2)] = odd
        return 0

    waited = set()

    def wait(*keys):
        for key in keys:
            if key in copies and key not in waited:
                copies[key].wait()
                waited.add(key)

    for k in range(CHUNKS):
        wait(*[(f, j) for j in (k - 1, k, k + 1) for f in range(2)], (2, k), (3, k))
        lax.fori_loop(k * per, (k + 1) * per, slab, 0, unroll=4)


def kernel_advect(
    places_h, tallies_h, rest, q_h, t_h, we_h, wn_h, parts_h,
    aq, at, table, cw, cs, radius, base, acc, leave_b, leave_a, straight_b, straight_a, along_y,
    qv, tv, wev, wnv, places, tallies, sems, psem,
):
    copies = [
        pltpu.make_async_copy(places_h, places, psem.at[0]),
        pltpu.make_async_copy(tallies_h, tallies, psem.at[2]),
        pltpu.make_async_copy(parts_h.at[0], radius, psem.at[1]),
    ]
    for c in copies:
        c.start()
    stencil(((q_h, qv), (t_h, tv), (we_h, wev), (wn_h, wnv)), sems, (aq, at, table))
    cw[...] = wev[0:CY] + 0.1
    cs[...] = wnv[pl.ds(0, CX, stride=CY)] + 0.1
    for c in copies:
        c.wait()

    def prepare(g, _):
        rows = pl.ds(pl.multiple_of(g * 64, 64), 64)
        base[rows] = growth_base(radius[rows], rest[1, rows])
        for k in range(LANES_ACC):
            acc[k, rows] = jnp.zeros((64, LEV), F32)
        return 0

    lax.fori_loop(0, NB // 64, prepare, 0, unroll=2)
    for leave, n, d in gx_sends((leave_b, leave_a)):
        fetch_rows(SLOTS, lambda s, d=d: places[0, 0, d, s], [(base, leave.at[n])])
    slot = lax.broadcasted_iota(jnp.int32, (SLOTS, LEV), 0)
    ox = odd_x()
    straight = (
        (straight_b, jnp.where(ox, EAST[0], WEST[0])), (straight_a, jnp.where(ox, WEST[0], EAST[0])),
        (along_y.at[0], NORTH[0]), (along_y.at[1], SOUTH[0]),
    )
    for pair, d in straight:
        for p in range(2):
            dst = pair.at[p]
            fetch_rows(SLOTS, lambda s, d=d: places[0, 0, d, s], [(rest.at[p], dst)])
            dst[...] = jnp.where(slot < tallies[0, 0, d], dst[...], 0.0)


def steer(sends, place, north, south, of_b, of_a):
    ox, oy = odd_x(), odd_y()
    for n in range(3):
        if n == 0:
            up, down = north, south
        else:
            one, two = (of_a, of_b) if n == 1 else (of_b, of_a)
            up = jnp.where(ox, one(1), two(1))
            down = jnp.where(ox, one(2), two(2))
        sends[0][place(n)] = jnp.where(oy, up, down)
        sends[1][place(n)] = jnp.where(oy, down, up)


def scatter_rows(home, cond, acc, start, stop):
    half = lax.broadcasted_iota(jnp.int32, (1, LEV), 1) // 64

    def scatter(g, _):
        b0 = g * LANES_ACC
        where = [home[b0 + k] for k in range(LANES_ACC)]
        rows = [pl.ds(c >> 1, 1) for c in where]
        sums = [
            acc[k, rows[k]] + jnp.where(half == (where[k] & 1), cond[pl.ds(b0 + k, 1)], 0.0)
            for k in range(LANES_ACC)
        ]
        for k in range(LANES_ACC):
            acc[k, rows[k]] = sums[k]
        return 0

    lax.fori_loop(start // LANES_ACC, stop // LANES_ACC, scatter, 0, unroll=UNROLL)


def kernel_fix(
    places_h, tallies_h, home_h, hxb, hxa, hyb, hya, cw, cs, leave_b, leave_a, straight_b, straight_a, along_y, aq_in, at_in, table_in,
    aq, at, table, send_b, send_a, rest_b, rest_a, got, places, tallies, home, sems,
):
    lists = ((places_h, places), (tallies_h, tallies), (home_h, home))
    copies = [pltpu.make_async_copy(a, b, sems.at[k]) for k, (a, b) in enumerate(lists)]
    for c in copies:
        c.start()
    ox, oy = odd_x(), odd_y()
    for f, a in ((0, aq), (1, at)):
        a[0:CY] += cw[...] * jnp.where(ox, hxa[f], hxb[f])
        a[ROWS - CY : ROWS] += 0.1 * jnp.where(ox, hxb[f], hxa[f])
        a[pl.ds(0, CX, stride=CY)] += cs[...] * jnp.where(oy, hya[f], hyb[f])
        a[pl.ds(CY - 1, CX, stride=CY)] += 0.1 * jnp.where(oy, hyb[f], hya[f])

    def refresh(rows, start, count, stride):
        even, odd = both_halves(supersat(aq[rows], at[rows]))
        table[pl.ds(2 * start, count, stride=2 * stride)] = even
        table[pl.ds(2 * start + 1, count, stride=2 * stride)] = odd

    refresh(pl.ds(0, CY), 0, CY, 1)
    refresh(pl.ds(ROWS - CY, CY), ROWS - CY, CY, 1)
    refresh(pl.ds(0, CX, stride=CY), 0, CX, CY)
    refresh(pl.ds(CY - 1, CX, stride=CY), CY - 1, CX, CY)
    for c in copies:
        c.wait()
    slot = lax.broadcasted_iota(jnp.int32, (SLOTS, LEV), 0)
    bases, straight = (leave_b, leave_a), (straight_b, straight_a)
    for k, (send, n, d) in enumerate(gx_sends((send_b, send_a))):
        fetch_rows(SLOTS, lambda s, d=d: home[places[0, 0, d, s]], [(table, got)])
        if n == 0:
            send[3], send[4] = straight[k // 3][0], straight[k // 3][1]
        square = bases[k // 3][n] + 20.0 * got[...]
        send[n] = jnp.where(slot < tallies[0, 0, d], root(jnp.maximum(square, 0.25)), 0.0)
    for p in range(2):
        steer(
            (rest_b, rest_a), lambda n, p=p: 2 * n + p, along_y[0, p], along_y[1, p],
            lambda n, p=p: hxb[2 * n + p], lambda n, p=p: hxa[2 * n + p],
        )


def kernel_grow(places, tallies, home, table, radius, rest, base, acc_in, parts_out, ahead, acc, cond, got, new_r, sems, psem):
    copies = [pltpu.make_async_copy(rest.at[p], parts_out.at[1 + p], psem.at[p]) for p in range(2)]
    for c in copies:
        c.start()
    outs = []
    per = NB // CHUNKS
    for k in range(CHUNKS):
        fetch_rows(per, lambda s, k=k: home[k * per + s], [(table, got.at[k % 2])], 128)

        def grow(g, _, k=k):
            here = pl.ds(pl.multiple_of(g * 64, 64), 64)
            rows = pl.ds(pl.multiple_of(k * per + g * 64, 64), 64)
            r, m = radius[rows], rest[0, rows]
            square = base[rows] + 20.0 * got[k % 2, here]
            square = jnp.maximum(square, 0.25)
            new = root(square)
            new_r[rows] = new
            taken = (0.0003 * m) * (square * new - r * r * r)
            cond[rows] = taken + pltpu.roll(taken, 64, 1)
            return 0

        lax.fori_loop(0, per // 64, grow, 0, unroll=4)
        c = pltpu.make_async_copy(
            new_r.at[pl.ds(k * per, per)], parts_out.at[0, pl.ds(k * per, per)], sems.at[k]
        )
        c.start()
        outs.append(c)
    slot = lax.broadcasted_iota(jnp.int32, (SLOTS, LEV), 0)
    for n, d in enumerate((2, 3)):
        dst = ahead.at[n]
        fetch_rows(SLOTS, lambda s, d=d: places[0, 0, d, s], [(new_r, dst)])
        dst[...] = jnp.where(slot < tallies[0, 0, d], dst[...], 0.0)
    scatter_rows(home, cond, acc, 0, NB)
    for c in outs + copies:
        c.wait()


def kernel_forward(ahead, ra, rb, yb, ya):
    steer((yb, ya), lambda n: n, ahead[0], ahead[1], lambda n: rb[n], lambda n: ra[n])


def kernel_deposit(aq, at, acc, q_out, t_out, qo, to, sems):
    outs = []
    for j in range(CHUNKS):

        def gather(g, _, j=j):
            rows = pl.ds(pl.multiple_of(j * CROWS + g * 64, 64), 64)
            dep = acc[0, rows]
            for k in range(1, LANES_ACC):
                dep = dep + acc[k, rows]
            qo[rows] = aq[rows] - dep
            to[rows] = at[rows] + 2.5 * dep
            return 0

        lax.fori_loop(0, CROWS // 64, gather, 0)
        for n, (src, dst) in enumerate(((qo, q_out), (to, t_out))):
            rows = pl.ds(j * CROWS, CROWS)
            c = pltpu.make_async_copy(src.at[rows], dst.at[rows], sems.at[n, j])
            c.start()
            outs.append(c)
    for c in outs:
        c.wait()


def kernel_arrive(ra, rb, yrb, yra, ymb, yma, out, buf, sems):
    ox, oy = odd_x(), odd_y()
    copies = []
    for d, odd, one, two, n, skip in (
        (0, ox, (ra, ra), (rb, rb), 0, 3), (1, ox, (rb, rb), (ra, ra), 0, 3),
        *((NORTH[n], oy, (yra, yma), (yrb, ymb), n, 0) for n in range(3)),
        *((SOUTH[n], oy, (yrb, ymb), (yra, yma), n, 0) for n in range(3)),
    ):
        buf[d, 0] = jnp.where(odd, one[0][n], two[0][n])
        for p in range(2):
            k = skip + 2 * n + p
            buf[d, 1 + p] = jnp.where(odd, one[1][k], two[1][k])
        copies.append(pltpu.make_async_copy(buf.at[d], out.at[d], sems.at[d]))
        copies[-1].start()
    for c in copies:
        c.wait()


def vmem(*shape):
    return pltpu.VMEM(shape, F32)


def hbm(*shape):
    return pltpu.HBM(shape, F32)


def in_hbm(x):
    return pltpu.with_memory_space_constraint(x, pltpu.HBM)


def dma(*shape):
    return pltpu.SemaphoreType.DMA(shape)


def call(kernel, name, us, ins, outs, shapes, scratch, aliases=None, mib=24):
    return pl.pallas_call(
        kernel,
        in_specs=ins,
        out_specs=outs,
        out_shape=shapes,
        scratch_shapes=scratch,
        input_output_aliases=aliases or {},
        compiler_params=pltpu.CompilerParams(vmem_limit_bytes=mib << 20),
        cost_estimate=pl.CostEstimate(flops=0, bytes_accessed=int(us * 3.0e6), transcendentals=0),
        name=name,
    )


def swapped(value, axis, phase):
    count = lax.axis_size(axis)
    step = [1 if (i + phase) % 2 == 0 else -1 for i in range(count)]
    return lax.ppermute(value, axis, [(i, (i + step[i]) % count) for i in range(count)])


def body(q, t, we, wn, parts, home, places, tallies):
    parts = in_hbm(parts.transpose(1, 0, 2))
    q_h, t_h = in_hbm(q), in_hbm(t)
    flat = [in_hbm(x.reshape(ROWS, LEV)) for x in (q, t, we, wn)]
    places_h, tallies_h, home_h = in_hbm(places), in_hbm(tallies), in_hbm(home)
    places_s, tallies_s = pltpu.SMEM((1, 1, 8, SLOTS), jnp.int32), pltpu.SMEM((1, 1, 8), jnp.int32)
    cells, table_of, blocks = vmem(ROWS, LEV), vmem(2 * ROWS, LEV), vmem(NB, LEV)
    pairs, radii = vmem(6, SLOTS, LEV), vmem(3, SLOTS, LEV)
    sums = vmem(LANES_ACC, ROWS, LEV)
    xb, xa, yb, ya, rest = call(
        kernel_send, "send_edges", 1, [ANY] * 5, [VM] * 5,
        [vmem(6, CY, LEV)] * 2 + [vmem(2, CX, LEV)] * 2 + [vmem(2, NB, LEV)],
        [vmem(2, 2, CY, LEV), vmem(2, 2, CX, 8, LEV), places_s, tallies_s, dma(2, 2), dma(2, 2), dma(4)],
    )(q_h, t_h, places_h, tallies_h, parts)
    hxb = swapped(xb, "gx", 1)
    hxa = swapped(xa, "gx", 0)
    hyb = swapped(yb, "gy", 1)
    hya = swapped(ya, "gy", 0)
    aq, at, table, cw, cs, radius, base, acc, leave_b, leave_a, straight_b, straight_a, along_y = call(
        kernel_advect, "advect", 6, [ANY] * 2 + [VM] + [ANY] * 5, [VM] * 13,
        [cells, cells, table_of, vmem(CY, LEV), vmem(CX, LEV), blocks, blocks, sums, radii, radii,
         vmem(2, SLOTS, LEV), vmem(2, SLOTS, LEV), vmem(2, 2, SLOTS, LEV)],
        [cells] * 4 + [places_s, tallies_s, dma(4, CHUNKS), dma(3)],
    )(places_h, tallies_h, rest, *flat, parts)
    aq, at, table, rb, ra, ymb, yma = call(
        kernel_fix, "fix_edges", 1, [ANY] * 3 + [VM] * 14, [VM] * 7,
        [cells, cells, table_of, vmem(5, SLOTS, LEV), vmem(5, SLOTS, LEV), pairs, pairs],
        [vmem(SLOTS, LEV), places_s, tallies_s, pltpu.SMEM((NB,), jnp.int32), dma(3)],
        {14: 0, 15: 1, 16: 2},
    )(places_h, tallies_h, home_h, hxb, hxa, hyb, hya, cw, cs, leave_b, leave_a, straight_b, straight_a, along_y,
      aq, at, table)
    rb = swapped(rb, "gx", 1)
    ra = swapped(ra, "gx", 0)
    ymb = swapped(ymb, "gy", 1)
    yma = swapped(yma, "gy", 0)
    parts_out, ahead, acc = call(
        kernel_grow, "grow", 6, [SM] * 3 + [VM] * 5, [ANY, VM, VM],
        [hbm(3, NB, LEV), vmem(2, SLOTS, LEV), sums],
        [blocks, vmem(2, NB // CHUNKS, LEV), blocks, dma(CHUNKS), dma(2)], {7: 2},
    )(places, tallies, home, table, radius, rest, base, acc)
    yb, ya = call(kernel_forward, "forward", 1, [VM] * 3, [VM] * 2, [radii, radii], [])(ahead, ra, rb)
    yrb = swapped(yb, "gy", 1)
    yra = swapped(ya, "gy", 0)
    q_out, t_out = call(
        kernel_deposit, "deposit", 4, [VM] * 3, [ANY, ANY],
        [hbm(ROWS, LEV), hbm(ROWS, LEV)], [cells, cells, dma(2, CHUNKS)],
    )(aq, at, acc)
    arrived = call(
        kernel_arrive, "arrive", 1, [VM] * 6, ANY, hbm(8, 3, SLOTS, LEV),
        [vmem(8, 3, SLOTS, LEV), dma(8)],
    )(ra, rb, yrb, yra, ymb, yma)
    incoming = arrived.transpose(0, 2, 1, 3)[None, None]
    shape = (CX, CY, LEV)
    return q_out.reshape(shape), t_out.reshape(shape), parts_out.transpose(1, 0, 2), incoming


def solution(mesh):
    cells = P("gx", "gy", None)
    blocks = P(("gx", "gy"), None, None)
    return jax.shard_map(
        body,
        mesh=mesh,
        in_specs=(cells, cells, cells, cells, blocks, P(("gx", "gy")),
                  P("gx", "gy", None, None), P("gx", "gy", None)),
        out_specs=(cells, cells, blocks, P("gx", "gy", None, None, None, None)),
        check_vma=False,
    )
```
